128 devices in a mesh: ctx: 4 (over z_hi, core), exp: 32 (over x, y, z_lo).
Axes of the slice: x: 4, y: 4, z: 4 (z_hi: 2, z_lo: 2; z = z_hi * 2 + z_lo), core: 2. Of those that a mesh axis runs over, the one named last changes fastest.
Arguments:
- resid: bfloat16 [2048, 4096], P(('ctx', 'exp')), may hold values from -6 to 6
- query: bfloat16 [2048, 8192], P('ctx', 'exp'), may hold values from -100 to 100
- keys: bfloat16 [2048, 512], P('ctx'), may hold values from -4 to 4
- values: bfloat16 [2048, 512], P('ctx'), may hold values from -8 to 8
- out_weight: bfloat16 [8192, 4096], P('exp'), may hold values from -0.0625 to 0.0625
- post_gain: float32 [4096], replicated, may hold values from 0.5 to 1.5
- route_idx: int32 [2048, 8], replicated, may hold values from 0 to 31, all different within a row; in each aligned block of 16 rows (0 to 15, 16 to 31, ...) at most 8 rows name the same one
- gates: float32 [2048, 8], P(('ctx', 'exp')), may hold values from 0.05 to 0.5
- w_gate: bfloat16 [32, 4096, 1536], P('exp', None, 'ctx'), may hold values from -0.09375 to 0.09375
- w_up: bfloat16 [32, 4096, 1536], P('exp', None, 'ctx'), may hold values from -0.09375 to 0.09375
- w_down: bfloat16 [32, 1536, 4096], P('exp', 'ctx'), may hold values from -0.15625 to 0.15625
Outputs:
- mixed: bfloat16 [2048, 4096], P(('ctx', 'exp'))
- attn_out: float32 [2048, 4096], P(('ctx', 'exp'))
- gram: float32 [32, 1536, 1536], P('exp', 'ctx')
The draws below stay inside these ranges and needn't reach their ends.
Inputs may be any that keep to these rules, and one draw needn't show every extreme that they name: `route_idx`: in each aligned block of 16 rows (the rows of one device) no expert is named by more than 8 rows, a bound that some block reaches.
All inputs are finite; a program needn't handle non-finite values.
Results may differ from the reference program's by a relative error of at most 0.03.
Values may be sent and summed in bfloat16 or wider, within the bound.
A program may use at most 128 MiB of HBM per device.

```python
import math
import jax
import jax.numpy as jnp
import numpy as np
from jax import lax

D = 4096
FF = 1536
QUERY_HEADS = 64
KEY_VALUE_HEADS = 4
HEAD_SIZE = 128
SEQUENCE_TOKENS = 2048
TOK_DEV = 16
EXPERTS = 32
TOP = 8
CAP = 8
N_CTX = 4
N_EXP = 32


def shared_keys(key):
    base_offset = jax.random.normal(jax.random.fold_in(key, 11), (SEQUENCE_TOKENS, KEY_VALUE_HEADS * HEAD_SIZE), jnp.float32)
    return jnp.clip(base_offset, -4.0, 4.0)


def draw_keys(key, part):
    base_offset = shared_keys(key)
    return base_offset.astype(jnp.bfloat16)


def draw_query(key, part):
    key = jax.random.fold_in(key, 5)
    fresh = jnp.clip(jax.random.normal(key, (SEQUENCE_TOKENS, QUERY_HEADS * HEAD_SIZE), jnp.float32), -4.0, 4.0)
    return fresh.astype(jnp.bfloat16)


def levels(own_key, shape, shards, least, top_value):
    loudness, own = 1.0, jax.random.fold_in(own_key, 6)
    for position, parts in shards:
        steps = jnp.exp(jax.random.uniform(jax.random.fold_in(own, position), (parts,), jnp.float32, least / len(shards), top_value / len(shards)))
        loudness = loudness * jnp.repeat(steps, shape[position] // parts).reshape([-1 if axis == position else 1 for axis in range(len(shape))])
    return loudness


def assign_block(own_key, own, number, rows, number_of, top, bound, skew):
    order = jax.random.permutation(own_key, number_of)
    crowded, common = portions_of(number_of, rows * top, bound, skew, True), portions_of(number_of, rows * top, bound, skew, False)
    places = jnp.arange(number_of)

    def named(tallies, offset_by):
        used = int((tallies > 0).sum())
        fixed = max(1, used // 4)
        passed = fixed + (places - fixed + offset_by * (used - fixed)) % max(1, number_of - fixed)
        return jnp.zeros((number_of,), jnp.int32).at[order[jnp.where(places < fixed, places, passed)]].set(jnp.asarray(tallies, jnp.int32))

    tallies = jnp.where(number % 4 == 0, named(crowded, number // 4), named(common, number - number // 4 - 1))
    mixed = jax.random.permutation(jax.random.fold_in(own, 3), number_of)
    source_of, receiver = mixed[0:number_of // 2 * 2:2], mixed[1:number_of // 2 * 2:2]
    slack = jnp.minimum(tallies[source_of] - 1, bound - tallies[receiver]) // 2
    slack = jnp.where((source_of == order[0]) | (receiver == order[0]) | (tallies[receiver] == 0), 0, jnp.maximum(slack, 0))
    passed = jax.random.randint(jax.random.fold_in(own, 4), (number_of // 2,), 0, 1 << 20) % (slack + 1)
    tallies = tallies.at[source_of].add(-passed).at[receiver].add(passed)
    labels = jnp.searchsorted(jnp.cumsum(tallies), jnp.arange(rows * top), side="right").astype(jnp.int32)
    listing = labels.reshape(top, rows).T
    listing = listing[jax.random.permutation(jax.random.fold_in(own, 1), rows)]
    offset_by = jax.random.randint(jax.random.fold_in(own, 2), (rows, 1), 0, top)
    return jnp.take_along_axis(listing, (jnp.arange(top)[None, :] + offset_by) % top, axis=1)


def portions_of(number_of, total, limit, skew, full):
    weights = [(1 << 20) // math.isqrt(grade ** skew) + 1 for grade in range(1, number_of + 1)]
    largest = limit if full else min(limit, max(-(-total // number_of), total * weights[0] // sum(weights)))
    least = 1 if total - largest >= number_of - 1 else 0
    given, surplus = [largest] + [least] * (number_of - 1), total - largest - least * (number_of - 1)
    while surplus > 0:
        free = [i for i in range(1, number_of) if given[i] < largest] or [i for i in range(1, number_of) if given[i] < limit]
        mass, budget = sum([weights[i] for i in free]), surplus
        for i in free:
            more = min(limit - given[i], max(1, budget * weights[i] // mass), surplus)
            given[i] = given[i] + more
            surplus = surplus - more
    return np.array(given)


def noise(stream_key, dims, deviation, reach, shards=(), dtype=jnp.bfloat16):
    values = jax.random.normal(stream_key, dims, jnp.float32) * deviation
    if len(shards) > 0:
        values = levels(stream_key, dims, shards, -0.22, 0.18) * values
    return jnp.clip(values, min=-reach, max=reach).astype(dtype)


def setup_inputs(seed: int = 0) -> dict:
    splits = jax.random.split(jax.random.key(seed), 12)
    resid = noise(splits[0], (SEQUENCE_TOKENS, D), 1.0, 6.0, ((0, 128),))
    query = draw_query(jax.random.fold_in(splits[11], 71), 0)
    keys = draw_keys(jax.random.fold_in(splits[11], 71), 0)
    values = noise(splits[3], (SEQUENCE_TOKENS, KEY_VALUE_HEADS * HEAD_SIZE), 2.0, 8.0, ((0, 4),))
    out_weight = noise(splits[4], (QUERY_HEADS * HEAD_SIZE, D), (QUERY_HEADS * HEAD_SIZE) ** -0.5, 0.0625, ((0, 32),))
    post_gain = jnp.clip(1.0 + 0.1 * jax.random.normal(splits[5], (D,), jnp.float32), 0.5, 1.5)
    route_idx_keys = jax.random.split(jax.random.fold_in(splits[6], 1), SEQUENCE_TOKENS // TOK_DEV)
    route_idx_turns = jax.random.permutation(jax.random.fold_in(splits[6], 3), SEQUENCE_TOKENS // TOK_DEV)
    route_idx = jax.vmap(lambda own, number: assign_block(jax.random.fold_in(splits[6], 2), own, number, TOK_DEV, EXPERTS, TOP, CAP, 2))(route_idx_keys, route_idx_turns).reshape((SEQUENCE_TOKENS, TOP))
    gates = jnp.clip(jnp.exp(math.log(0.5) - 2.3025851 * jax.random.uniform(splits[7], (SEQUENCE_TOKENS, TOP), jnp.float32) ** levels(splits[7], (SEQUENCE_TOKENS, TOP), ((0, 128),), -0.2, 0.2)), 0.05, 0.5)
    w_gate = noise(splits[8], (EXPERTS, D, FF), D ** -0.5, 0.09375, ((0, 32), (2, 4)))
    w_up = noise(splits[9], (EXPERTS, D, FF), D ** -0.5, 0.09375, ((0, 32), (2, 4)))
    w_down = noise(splits[10], (EXPERTS, FF, D), FF ** -0.5, 0.15625, ((0, 32), (1, 4)))
    return {"resid": resid, "query": query, "keys": keys, "values": values, "out_weight": out_weight, "post_gain": post_gain, "route_idx": route_idx, "gates": gates, "w_gate": w_gate, "w_up": w_up, "w_down": w_down}


def attention_heads(query, keys, values):
    head_group = QUERY_HEADS // KEY_VALUE_HEADS
    scale = 1.0 / math.sqrt(HEAD_SIZE)
    place = jnp.arange(SEQUENCE_TOKENS).astype(jnp.int32)
    causal = place[:, None] >= place[None, :]

    def one_head(head):
        kv_head = head // head_group
        q_part = lax.dynamic_slice_in_dim(query, (head * HEAD_SIZE).astype(jnp.int32), HEAD_SIZE, 1)
        k_part = lax.dynamic_slice_in_dim(keys, (kv_head * HEAD_SIZE).astype(jnp.int32), HEAD_SIZE, 1)
        v_part = lax.dynamic_slice_in_dim(values, (kv_head * HEAD_SIZE).astype(jnp.int32), HEAD_SIZE, 1)
        scores = jnp.dot(q_part, k_part.T, preferred_element_type=jnp.float32) * scale
        scores = jnp.where(causal, scores, -jnp.inf)
        peak = lax.optimization_barrier(jnp.max(scores, axis=1, keepdims=True))
        weights = jnp.where(causal, jnp.exp(scores - peak), 0.0).astype(jnp.bfloat16)
        total = lax.optimization_barrier(jnp.sum(weights.astype(jnp.float32), axis=1, keepdims=True))
        mixed_v = jnp.dot(weights, v_part, preferred_element_type=jnp.float32)
        return (mixed_v / total).astype(jnp.bfloat16)
    heads = lax.map(one_head, jnp.arange(QUERY_HEADS).astype(jnp.int32))
    return jnp.transpose(heads, (1, 0, 2)).reshape(SEQUENCE_TOKENS, QUERY_HEADS * HEAD_SIZE)

def reference(resid, query, keys, values, out_weight, post_gain, route_idx, gates, w_gate, w_up, w_down):
    heads = attention_heads(query, keys, values)
    attn_out = jnp.dot(heads, out_weight, preferred_element_type=jnp.float32)
    stream = (resid.astype(jnp.float32) + attn_out).astype(jnp.bfloat16)
    stream_f = stream.astype(jnp.float32)
    normed = (stream_f * lax.rsqrt(lax.optimization_barrier(jnp.mean(stream_f * stream_f, axis=1, keepdims=True)) + 1e-06) * post_gain).astype(jnp.bfloat16)
    member = jnp.any(route_idx[:, :, None] == jnp.arange(EXPERTS).astype(jnp.int32)[None, None, :], axis=1)
    member_i = member.astype(jnp.int32)
    counts = lax.optimization_barrier(jnp.sum(member_i, axis=0))
    ranks = jnp.cumsum(member_i, axis=0) - 1
    most_rows = N_CTX * N_EXP * CAP
    padded = jnp.concatenate([normed, jnp.zeros((1, D), jnp.bfloat16)], axis=0)

    def one_expert(expert):
        chosen = jnp.nonzero(member[:, expert], size=most_rows, fill_value=SEQUENCE_TOKENS)[0].astype(jnp.int32)
        rows = padded[chosen]
        gate = jnp.dot(rows, w_gate[expert], preferred_element_type=jnp.float32)
        upper = jnp.dot(rows, w_up[expert], preferred_element_type=jnp.float32)
        hidden = (jax.nn.silu(gate) * upper).astype(jnp.bfloat16)
        gram_e = jnp.dot(hidden.T, hidden, preferred_element_type=jnp.float32) / counts[expert].astype(jnp.float32)
        out_rows = jnp.dot(hidden, w_down[expert], preferred_element_type=jnp.float32).astype(jnp.bfloat16)
        return (gram_e, out_rows)
    gram, out_rows = lax.map(one_expert, jnp.arange(EXPERTS).astype(jnp.int32))
    place = jnp.take_along_axis(ranks, route_idx, axis=1)
    selected_experts = out_rows[route_idx, place]
    routed = lax.optimization_barrier(jnp.sum(gates[:, :, None] * selected_experts.astype(jnp.float32), axis=1))
    mixed = (stream_f + routed).astype(jnp.bfloat16)
    return (mixed, attn_out, gram)
```

```python
import functools
import math

import jax
import jax.numpy as jnp
from jax import lax
from jax.experimental import pallas as pl
from jax.experimental.pallas import tpu as pltpu
from jax.sharding import PartitionSpec as P

QUERY_HEADS = 64
EXPERTS = 32
KEY_VALUE_HEADS = 4
HEAD_SIZE = 128
D = 4096
FF = 1536
FFS = 384
HALF = D // 2
QUART = D // 4
MESH = pl.DeviceIdType.MESH
BF = jnp.bfloat16
F32 = jnp.float32

RS_ORDER = ((0, 2, 1, 3, 4), (2, 1, 3, 0, 4), (1, 3, 0, 2, 4), (3, 0, 2, 1, 4))
CYCLE = (0, 2, 4, 1, 3, 5)
WIDTHS = (384, 384, 384, 384, 384, 256)
USED = (384, 384, 384, 384, 256, 256)
OFFS = (0, 384, 768, 1152, 1536, 1792)
WIDE = HALF + 128
GRAY = (0, 1, 3, 2)
ZMAP = ((0, 0), (1, 0), (1, 1), (0, 1))
FULL = slice(None)


def block_bits(i, n):
    return [(i // (2 ** (n - 1 - j))) % 2 for j in range(n)]


def kernel(
    h_ref, ow_ref, resid_ref, gain_ref, gate_ref, sel_ref, exp_ref, wg_ref, wu_ref, wd_ref,
    mixed_ref, attn_ref, gram_ref,
    p1, r10, r11, r12, r13, r14, norm, stream, csh, x0, x1, x2, x3, x4, x5,
    wgk, wuk, wgs, wus, wdq, xs, psend, precv, hall, p2, r20, r21, r22, r23, r24, fsend, frecv,
    s1s, s1r, wss, wsr, lsem, ccs, ccr, ags, agr, pss, psr, hss, hsr, s2s, s2r, fss, fsr,
):
    c = lax.axis_index("ctx")
    e = lax.axis_index("exp")
    x, y, zl, zh, k = e // 8, (e // 2) % 4, e % 2, c // 2, c % 2

    def dev(x_, y_, zl_, zh_, k_):
        return (zh_ * 2 + k_, x_ * 8 + y_ * 2 + zl_)

    def flip1(v):
        return v + 1 - 2 * (v % 2)

    peer_x = (dev(3 - x, y, zl, zh, k), dev(flip1(x), y, zl, zh, k))
    peer_y = (dev(x, 3 - y, zl, zh, k), dev(x, flip1(y), zl, zh, k))
    peer_z1 = dev(x, y, 1 - zl, zh, k)
    peer_z3 = dev(x, y, 1 - zl, 1 - zh, k)
    sib = dev(x, y, zl, zh, 1 - k)
    far = dev(x, y, zl, 1 - zh, k)
    farsib = dev(x, y, zl, 1 - zh, 1 - k)
    rs_peer = (peer_x[0], peer_x[1], peer_y[0], peer_y[1], peer_z1)
    ag_peer = (peer_x[0], peer_x[1], peer_y[0], peer_y[1], peer_z3, peer_z1)
    xb1, yb1 = x // 2, y // 2
    own5 = (xb1, (xb1 + x % 2) % 2, yb1, (yb1 + y % 2) % 2, zl)
    own6 = own5[:4] + (zh, (zh + zl) % 2)

    barrier = pltpu.get_barrier_semaphore()
    partners = list(ag_peer) + [sib, far, farsib]
    for p in partners:
        pl.semaphore_signal(barrier, inc=1, device_id=p, device_id_type=MESH)
    pl.semaphore_wait(barrier, len(partners))

    def remote(src, dst, ss, rs, to):
        return pltpu.make_async_remote_copy(
            src_ref=src, dst_ref=dst, send_sem=ss, recv_sem=rs, device_id=to, device_id_type=MESH
        )

    def rs_index(f, s, bit):
        order = RS_ORDER[f]
        idx = [FULL] * 5
        for d in order[:s]:
            idx[d] = own5[d]
        idx[order[s]] = bit
        return tuple(idx)

    def rs_copy(buf, recv, ss, rs, f, s):
        d = RS_ORDER[f][s]
        return remote(
            buf.at[(f,) + rs_index(f, s, 1 - own5[d])], recv[s].at[f], ss.at[f, s], rs.at[f, s], rs_peer[d]
        )

    def rs_add(buf, recv, f, s):
        order = RS_ORDER[f]
        left = sorted(order[s + 1 :])
        n = len(left)

        def one(i):
            bits = block_bits(i, n)
            idx = list(own5)
            for d, b in zip(left, bits):
                idx[d] = b
            idx = (f,) + tuple(idx)
            got = recv[s][(f,) + tuple(bits)]
            buf[idx] = (buf[idx].astype(F32) + got.astype(F32)).astype(BF)

        pl.loop(0, 2**n)(one)

    recv1 = (r10, r11, r12, r13, r14)
    recv2 = (r20, r21, r22, r23, r24)

    def project(f, bit):
        idx = rs_index(f, 0, bit)
        rows = h_ref[idx].reshape(256, 256)
        for t in range(2):
            cols = f * 1024 + t * 512
            out = jnp.dot(rows, ow_ref[:, cols : cols + 512], preferred_element_type=F32)
            p1[(f,) + idx + (FULL, slice(t * 512, t * 512 + 512))] = out.astype(BF).reshape(2, 2, 2, 2, 16, 512)

    first = []
    for f in range(4):
        project(f, 1 - own5[RS_ORDER[f][0]])
        cp = rs_copy(p1, recv1, s1s, s1r, f, 0)
        cp.start()
        first.append(cp)

    other = pl.ds(pl.multiple_of((1 - k) * HALF, HALF), HALF)
    mine = pl.ds(pl.multiple_of(k * HALF, HALF), HALF)
    own_rows = pl.ds(pl.multiple_of(c * FFS, FFS), FFS)

    def quarter(cc):
        return pl.ds(pl.multiple_of(cc * QUART, QUART), QUART)

    weight_copies = [
        remote(wg_ref.at[other], wgs, wss.at[0], wsr.at[0], sib),
        remote(wu_ref.at[other], wus, wss.at[1], wsr.at[1], sib),
        remote(wd_ref.at[:, quarter(zh * 2 + 1 - k)], wdq.at[own_rows], wss.at[2], wsr.at[2], sib),
        remote(wd_ref.at[:, quarter((1 - zh) * 2 + k)], wdq.at[own_rows], wss.at[3], wsr.at[3], far),
        remote(wd_ref.at[:, quarter((1 - zh) * 2 + 1 - k)], wdq.at[own_rows], wss.at[4], wsr.at[4], farsib),
    ]
    local_copies = [
        pltpu.make_async_copy(wg_ref.at[mine], wgk, lsem.at[0]),
        pltpu.make_async_copy(wu_ref.at[mine], wuk, lsem.at[1]),
        pltpu.make_async_copy(wd_ref.at[:, quarter(c)], wdq.at[own_rows], lsem.at[2]),
    ]
    for cp in weight_copies + local_copies:
        cp.start()

    for f in range(4):
        project(f, own5[RS_ORDER[f][0]])

    def finish_rs(buf, recv, ss, rs, first):
        last = list(first)
        for s in range(4):
            for f in range(4):
                last[f].wait()
                rs_add(buf, recv, f, s)
                last[f] = rs_copy(buf, recv, ss, rs, f, s + 1)
                last[f].start()
        out = []
        for f in range(4):
            last[f].wait()
            out.append(buf[(f,) + own5].astype(F32) + recv[4][f].astype(F32))
        return out

    parts = finish_rs(p1, recv1, s1s, s1r, first)

    squares = jnp.zeros((16, 1), F32)
    for f in range(4):
        cols = slice(f * 1024, f * 1024 + 1024)
        attn_ref[:, cols] = parts[f]
        st = (resid_ref[:, cols].astype(F32) + parts[f]).astype(BF)
        stream[:, cols] = st
        sf = st.astype(F32)
        squares = squares + jnp.sum(sf * sf, axis=1, keepdims=True)
    inv = lax.rsqrt(squares / D + 1e-06)
    for f in range(4):
        cols = slice(f * 1024, f * 1024 + 1024)
        out = (stream[:, cols].astype(F32) * inv * gain_ref[:, cols]).astype(BF)
        norm[f // 2, :, (f % 2) * 1024 : (f % 2) * 1024 + 1024] = out
    gates = gate_ref[...]
    top = gates.astype(BF)
    rest = gates - top.astype(F32)
    middle = rest.astype(BF)
    low = (rest - middle.astype(F32)).astype(BF)
    lane = lax.broadcasted_iota(jnp.int32, (16, 128), 1)
    gates = jnp.where(lane < EXPERTS, top.astype(F32), jnp.where(lane < 2 * EXPERTS, middle.astype(F32), low.astype(F32)))
    for i in range(2):
        norm[i, :, HALF:] = gates.astype(BF)

    xf = (x0, x1, x2, x3, x4, x5)
    swap = remote(norm.at[1 - k], csh, ccs.at[0], ccr.at[0], sib)
    swap.start()
    own_tok = pl.ds(pl.multiple_of(k * 16, 16), 16)
    sib_tok = pl.ds(pl.multiple_of((1 - k) * 16, 16), 16)
    for f in range(6):
        xf[f][own6 + (own_tok, slice(0, USED[f]))] = norm[k, :, OFFS[f] : OFFS[f] + USED[f]]
    x4[own6 + (own_tok, slice(256, 384))] = norm[k, :, HALF:]
    swap.wait()
    for f in range(6):
        xf[f][own6 + (sib_tok, slice(0, USED[f]))] = csh[:, OFFS[f] : OFFS[f] + USED[f]]
    x4[own6 + (sib_tok, slice(256, 384))] = csh[:, HALF:]

    def ag_copy(f, s):
        done = [CYCLE[(f + t) % 6] for t in range(s)]
        d = CYCLE[(f + s) % 6]
        idx = tuple(FULL if j in done else own6[j] for j in range(6))
        return remote(xf[f].at[idx], xf[f].at[idx], ags.at[f, s], agr.at[f, s], ag_peer[d])

    last = []
    for f in range(6):
        cp = ag_copy(f, 0)
        cp.start()
        last.append(cp)
    for s in range(1, 6):
        for f in range(6):
            last[f].wait()
            last[f] = ag_copy(f, s)
            last[f].start()
    for f in range(6):
        last[f].wait()

    def select(g):
        b = block_bits(g, 3)
        pick = sel_ref[g]
        rows = pl.ds(pl.multiple_of(g * 128, 128), 128)
        for f in range(6):
            block = xf[f][tuple(b)].reshape(256, WIDTHS[f])[:, : USED[f]]
            xs[rows, OFFS[f] : OFFS[f] + USED[f]] = jnp.dot(pick, block, preferred_element_type=F32).astype(BF)

    pl.loop(0, 8)(select)
    for cp in weight_copies + local_copies:
        cp.wait()

    def partial_copy(m):
        return remote(psend.at[m], precv.at[m], pss.at[m], psr.at[m], sib)

    def other_units(m):
        a = xs[pl.ds(pl.multiple_of(m * 256, 256), 256), :]
        psend[m, :, :FFS] = jnp.dot(a, wgs[...], preferred_element_type=F32).astype(BF)
        psend[m, :, FFS:] = jnp.dot(a, wus[...], preferred_element_type=F32).astype(BF)
        partial_copy(m).start()

    pl.loop(0, 4)(other_units)

    def hidden_cols(cc):
        return pl.ds(pl.multiple_of(cc * FFS, 128), FFS)

    def hidden_copy(m, cc, kind, to):
        part = hall.at[pl.ds(pl.multiple_of(m * 256, 256), 256), hidden_cols(cc)]
        return remote(part, part, hss.at[kind, m], hsr.at[kind, m], to)

    def own_units(m):
        rows = pl.ds(pl.multiple_of(m * 256, 256), 256)
        a = xs[rows, :]
        gate = jnp.dot(a, wgk[...], preferred_element_type=F32)
        upper = jnp.dot(a, wuk[...], preferred_element_type=F32)
        partial_copy(m).wait()
        gate = gate + precv[m, :, :FFS].astype(F32)
        upper = upper + precv[m, :, FFS:].astype(F32)
        hall[rows, hidden_cols(c)] = (gate / (1.0 + jnp.exp(-gate)) * upper).astype(BF)
        hidden_copy(m, c, 0, far).start()
        hidden_copy(m, c, 1, sib).start()

    pl.loop(0, 4)(own_units)
    far_c = (1 - zh) * 2 + k

    def forward(m):
        hidden_copy(m, c, 0, far).wait()
        hidden_copy(m, far_c, 2, sib).start()

    pl.loop(0, 4)(forward)

    def down(m):
        hidden_copy(m, c, 1, sib).wait()
        hidden_copy(m, far_c, 2, sib).wait()
        rows = pl.ds(pl.multiple_of(m * 256, 256), 256)
        a = hall[rows, :]
        b1, b0 = m // 2, m % 2
        lane = lax.broadcasted_iota(jnp.int32, (256, 128), 1)
        mine = jnp.logical_or(lane == e, jnp.logical_or(lane == e + EXPERTS, lane == e + 2 * EXPERTS))
        weights = []
        for g in range(2):
            block = x4[b1, b0, g].reshape(256, 384)[:, 256:].astype(F32)
            weights.append(jnp.sum(jnp.where(mine, block, 0.0), axis=1, keepdims=True))
        for f in range(4):
            cols = slice(f * 256, f * 256 + 256)
            out = jnp.dot(a, wdq[:, cols], preferred_element_type=F32).astype(BF)
            for g in range(2):
                tok = jnp.dot(exp_ref[m * 2 + g], out[g * 128 : g * 128 + 128], preferred_element_type=F32)
                tok = (tok * weights[g]).astype(BF)
                for yb in range(2):
                    for j in range(4):
                        zlo, zhi = ZMAP[j]
                        at = (yb * 4 + j) * 32
                        p2[f, b1, b0, g, yb, zlo, zhi * 32 : zhi * 32 + 32, :] = tok[at : at + 32]

    pl.loop(0, 4)(down)

    first = []
    for f in range(4):
        cp = rs_copy(p2, recv2, s2s, s2r, f, 0)
        cp.start()
        first.append(cp)

    def gram(j):
        cols = pl.ds(pl.multiple_of(j * 256, 256), 256)
        gram_ref[:, cols] = lax.dot_general(
            hall[:, hidden_cols(c)], hall[:, cols], (((0,), (0,)), ((), ())), preferred_element_type=F32
        )

    pl.loop(0, 6)(gram)

    parts = finish_rs(p2, recv2, s2s, s2r, first)
    for f in range(4):
        cols = slice(f * 256, f * 256 + 256)
        fsend[:, :, cols] = parts[f].astype(BF).reshape(4, 16, 256)
    final = []
    for i, (cc, to) in enumerate(
        ((zh * 2 + 1 - k, sib), ((1 - zh) * 2 + k, far), ((1 - zh) * 2 + 1 - k, farsib))
    ):
        cp = remote(fsend.at[cc], frecv.at[c], fss.at[i], fsr.at[i], to)
        cp.start()
        final.append(cp)
    frecv[c] = fsend[c]
    for cp in final:
        cp.wait()
    for cc in range(4):
        cols = slice(cc * QUART, cc * QUART + QUART)
        mixed_ref[:, cols] = (stream[:, cols].astype(F32) + frecv[cc].astype(F32)).astype(BF)


def fused(h, ow, resid, gain, gate, sel, exp, wg, wu, wd):
    dma = pltpu.SemaphoreType.DMA
    vm = pl.BlockSpec(memory_space=pltpu.VMEM)
    hbm = pl.BlockSpec(memory_space=pl.ANY)
    two = (2,) * 6

    def rs_scratch(rows, cols):
        out = [pltpu.VMEM((4,) + (2,) * 5 + (rows, cols), BF)]
        for s in range(5):
            out.append(pltpu.VMEM((4,) + (2,) * (4 - s) + (rows, cols), BF))
        return out

    scratch = (
        rs_scratch(16, 1024)
        + [pltpu.VMEM((2, 16, WIDE), BF), pltpu.VMEM((16, D), BF), pltpu.VMEM((16, WIDE), BF)]
        + [pltpu.VMEM(two + (32, w), BF) for w in WIDTHS]
        + [pltpu.VMEM((HALF, FFS), BF)] * 4
        + [pltpu.VMEM((FF, QUART), BF), pltpu.VMEM((1024, HALF), BF)]
        + [pltpu.VMEM((4, 256, 2 * FFS), BF)] * 2
        + [pltpu.VMEM((1024, FF), BF)]
        + rs_scratch(64, 256)
        + [pltpu.VMEM((4, 16, QUART), BF)] * 2
        + [dma((4, 5)), dma((4, 5)), dma((5,)), dma((5,)), dma((3,)), dma((1,)), dma((1,))]
        + [dma((6, 6)), dma((6, 6)), dma((4,)), dma((4,)), dma((3, 4)), dma((3, 4))]
        + [dma((4, 5)), dma((4, 5)), dma((3,)), dma((3,))]
    )
    return pl.pallas_call(
        kernel,
        out_shape=(
            jax.ShapeDtypeStruct((16, D), BF),
            jax.ShapeDtypeStruct((16, D), F32),
            jax.ShapeDtypeStruct((FFS, FF), F32),
        ),
        in_specs=[vm] * 7 + [hbm] * 3,
        out_specs=(vm, vm, vm),
        scratch_shapes=scratch,
        compiler_params=pltpu.CompilerParams(
            collective_id=0, has_side_effects=True, vmem_limit_bytes=62 * 2**20
        ),
        name="layer",
    )(h, ow, resid, gain, gate, sel, exp, wg, wu, wd)


def gray(a, axis):
    parts = [lax.slice_in_dim(a, i, i + 1, axis=axis) for i in GRAY]
    return jnp.concatenate(parts, axis=axis)


def gathered_order(a):
    rest = a.shape[1:]
    n = len(rest)
    a = a.reshape((2, 2, 4, 4, 2, 16) + rest)
    a = jnp.transpose(a, (2, 3, 0, 4, 1, 5) + tuple(range(6, 6 + n)))
    a = a.reshape((4, 4, 4, 32) + rest)
    for axis in range(3):
        a = gray(a, axis)
    return a.reshape((2048,) + rest)


def attention(query, keys, values):
    ctx_pos = lax.axis_index("ctx")
    exp_pos = lax.axis_index("exp")
    span = query.shape[0]
    heads = query.shape[1] // HEAD_SIZE
    head_group = QUERY_HEADS // KEY_VALUE_HEADS
    scale = 1.0 / math.sqrt(HEAD_SIZE)
    kv_head = exp_pos * heads // head_group
    key_part = lax.dynamic_slice_in_dim(keys, kv_head * HEAD_SIZE, HEAD_SIZE, 1)
    value_part = lax.dynamic_slice_in_dim(values, kv_head * HEAD_SIZE, HEAD_SIZE, 1)
    both = jnp.concatenate([key_part, value_part], axis=1)
    both = lax.all_gather(both, "ctx", axis=0, tiled=True)
    k_piece, v_piece = both[:, :HEAD_SIZE], both[:, HEAD_SIZE:]
    q_heads = query.reshape(span, heads, HEAD_SIZE)
    q_place = ctx_pos * span + jnp.arange(span, dtype=jnp.int32)
    scores = jnp.einsum("qhd,kd->hqk", q_heads, k_piece, preferred_element_type=F32) * scale
    k_place = jnp.arange(k_piece.shape[0], dtype=jnp.int32)
    allowed = (q_place[:, None] >= k_place[None, :])[None]
    scores = jnp.where(allowed, scores, -1e30)
    peak = jnp.max(scores, axis=2)
    weights = jnp.where(allowed, jnp.exp(scores - peak[:, :, None]), 0.0).astype(BF)
    total = jnp.sum(weights.astype(F32), axis=2)
    accum = jnp.einsum("hqk,kd->qhd", weights, v_piece, preferred_element_type=F32)
    return (accum / total.T[:, :, None]).astype(BF).reshape(span, heads * HEAD_SIZE)


def local(
    resid, query, keys, values, out_weight, post_gain, route_idx, gates, w_gate, w_up, w_down
):
    exp_pos = lax.axis_index("exp")
    block = lax.axis_index("ctx") * EXPERTS + exp_pos
    own_idx = lax.dynamic_slice_in_dim(route_idx, block * 16, 16, 0)
    expert = jnp.arange(128, dtype=jnp.int32)
    expert = jnp.where(expert < 3 * EXPERTS, expert % EXPERTS, -1)
    gate = jnp.sum(jnp.where(own_idx[:, :, None] == expert[None, None, :], gates[:, :, None], 0.0), axis=1)
    head_rows = attention(query, keys, values)
    h = head_rows.reshape(4, 4, 32, 256)
    h = gray(gray(h, 0), 1).reshape(2, 2, 2, 2, 2, 16, 256)

    member = jnp.any(route_idx == exp_pos, axis=1)
    count = jnp.sum(member.astype(F32))
    member = gathered_order(member.astype(BF)).reshape(128, 16)
    before = (jnp.arange(16)[:, None] < jnp.arange(16)[None, :]).astype(BF)
    rank = jnp.dot(member, before, preferred_element_type=F32)
    rank = jnp.where(member > 0, rank, -1.0).astype(jnp.int32).reshape(8, 1, 256)
    slot = jnp.arange(128, dtype=jnp.int32)[None, :, None]
    token = jnp.arange(256, dtype=jnp.int32)[None, None, :]
    sel = jnp.logical_and(slot // 8 == token // 16, slot % 8 == rank)
    exp = jnp.transpose(sel, (0, 2, 1)).astype(BF)
    sel = sel.astype(BF)

    mixed, attn_out, gram = fused(
        h, out_weight, resid, post_gain.reshape(1, D), gate, sel, exp, w_gate[0], w_up[0], w_down[0]
    )
    return (mixed, attn_out, (gram / count)[None])


def solution(mesh):
    placed = (
        P(("ctx", "exp"), None),
        P("ctx", "exp"),
        P("ctx", None),
        P("ctx", None),
        P("exp", None),
        P(),
        P(),
        P(("ctx", "exp"), None),
        P("exp", None, "ctx"),
        P("exp", None, "ctx"),
        P("exp", "ctx", None),
    )
    return jax.shard_map(
        local,
        mesh=mesh,
        in_specs=placed,
        out_specs=(P(("ctx", "exp"), None), P(("ctx", "exp"), None), P("exp", "ctx", None)),
        check_vma=False,
    )
```

```python
import functools
import math

import jax
import jax.numpy as jnp
from jax import lax
from jax.experimental import pallas as pl
from jax.experimental.pallas import tpu as pltpu
from jax.sharding import PartitionSpec as P

EXPERTS = 32
HEAD_SIZE = 128
D = 4096
FF = 1536
FFS = 384
HALF = D // 2
QUART = D // 4
MESH = pl.DeviceIdType.MESH
BF = jnp.bfloat16
F32 = jnp.float32

RS_ORDER = ((0, 2, 1, 3, 4), (2, 1, 3, 0, 4), (1, 3, 0, 2, 4), (3, 0, 2, 1, 4))
CYCLE = (0, 2, 4, 1, 3, 5)
WIDTHS = (384, 384, 384, 384, 384, 256)
USED = (384, 384, 384, 384, 256, 256)
OFFS = (0, 384, 768, 1152, 1536, 1792)
WIDE = HALF + 128
GRAY = (0, 1, 3, 2)
ZMAP = ((0, 0), (1, 0), (1, 1), (0, 1))
FULL = slice(None)


def block_bits(i, n):
    return [(i // (2 ** (n - 1 - j))) % 2 for j in range(n)]


def kernel(
    q_ref, ow_ref, resid_ref, gain_ref, gate_ref, rank_ref, keys_ref, values_ref, wg_ref, wu_ref, wd_ref,
    mixed_ref, attn_ref, gram_ref,
    kv, top_s, sum_s, acc_s, h_ref, sel_ref,
    p1, r10, r11, r12, r13, r14, norm, stream, csh, x0, x1, x2, x3, x4, x5,
    wgk, wuk, wgs, wus, wdq, xs, psend, precv, hall, p2, r20, r21, r22, r23, r24, fsend, frecv,
    kvl, kvs, kvr,
    s1s, s1r, wss, wsr, lsem, ccs, ccr, ags, agr, pss, psr, hss, hsr, has, har, s2s, s2r, fss, fsr,
):
    c = lax.axis_index("ctx")
    e = lax.axis_index("exp")
    x, y, zl, zh, k = e // 8, (e // 2) % 4, e % 2, c // 2, c % 2

    def dev(x_, y_, zl_, zh_, k_):
        return (zh_ * 2 + k_, x_ * 8 + y_ * 2 + zl_)

    def flip1(v):
        return v + 1 - 2 * (v % 2)

    peer_x = (dev(3 - x, y, zl, zh, k), dev(flip1(x), y, zl, zh, k))
    peer_y = (dev(x, 3 - y, zl, zh, k), dev(x, flip1(y), zl, zh, k))
    peer_z1 = dev(x, y, 1 - zl, zh, k)
    peer_z3 = dev(x, y, 1 - zl, 1 - zh, k)
    sib = dev(x, y, zl, zh, 1 - k)
    far = dev(x, y, zl, 1 - zh, k)
    farsib = dev(x, y, zl, 1 - zh, 1 - k)
    rs_peer = (peer_x[0], peer_x[1], peer_y[0], peer_y[1], peer_z1)
    ag_peer = (peer_x[0], peer_x[1], peer_y[0], peer_y[1], peer_z3, peer_z1)
    xb1, yb1 = x // 2, y // 2
    own5 = (xb1, (xb1 + x % 2) % 2, yb1, (yb1 + y % 2) % 2, zl)
    own6 = own5[:4] + (zh, (zh + zl) % 2)

    barrier = pltpu.get_barrier_semaphore()
    partners = list(ag_peer) + [sib, far, farsib]
    for p in partners:
        pl.semaphore_signal(barrier, inc=1, device_id=p, device_id_type=MESH)
    pl.semaphore_wait(barrier, len(partners))

    def remote(src, dst, ss, rs, to):
        return pltpu.make_async_remote_copy(
            src_ref=src, dst_ref=dst, send_sem=ss, recv_sem=rs, device_id=to, device_id_type=MESH
        )

    head_cols = pl.ds(pl.multiple_of(x * HEAD_SIZE, HEAD_SIZE), HEAD_SIZE)
    kv_src = (keys_ref.at[:, head_cols], values_ref.at[:, head_cols])

    def kv_copy(i, to, cc, j):
        return remote(kv_src[j], kv.at[cc, j], kvs.at[i, j], kvr.at[cc, j], to)

    for j in range(2):

        @pl.when(zh == 0)
        def _():
            kv_copy(1, far, c, j).start()
            kv_copy(2, farsib, c, j).start()

    for j in range(2):

        @pl.when(k == 0)
        def _():
            kv_copy(0, sib, c, j).start()

        pltpu.make_async_copy(kv_src[j], kv.at[c, j], kvl.at[j]).start()

    slot = lax.broadcasted_iota(jnp.int32, (128, 256), 0)
    token = lax.broadcasted_iota(jnp.int32, (128, 256), 1)
    place = jnp.where(slot // 8 == token // 16, slot % 8, -2)

    def pick_slots(g):
        sel_ref[g] = jnp.where(place == rank_ref[g], 1.0, 0.0).astype(BF)

    pl.loop(0, 8)(pick_slots)
    top_s[...] = jnp.full((4, 256, 1), -1e30, F32)
    sum_s[...] = jnp.zeros((4, 256, 1), F32)
    acc_s[...] = jnp.zeros((4, 256, HEAD_SIZE), F32)
    for j in range(2):
        pltpu.make_async_copy(kv_src[j], kv.at[c, j], kvl.at[j]).wait()
    q_place = lax.rem(lax.broadcasted_iota(jnp.int32, (256, 512), 0), 128)
    k_place = lax.broadcasted_iota(jnp.int32, (256, 512), 1)
    scale = 1.0 / math.sqrt(HEAD_SIZE)

    def key_block(i):
        cc = c - i

        @pl.when(i > 0)
        def _():
            for j in range(2):
                kv_copy(0, sib, cc, j).wait_recv()

        def tile(t):
            rows = pl.ds(pl.multiple_of(t * 128, 128), 128)
            q = jnp.concatenate([q_ref[rows, :HEAD_SIZE], q_ref[rows, HEAD_SIZE:]], axis=0)
            scores = lax.dot_general(q, kv[cc, 0], (((1,), (1,)), ((), ())), preferred_element_type=F32) * scale
            allowed = q_place + (t * 128 + i * 512) >= k_place
            scores = jnp.where(allowed, scores, -1e30)
            old = top_s[t]
            new = jnp.maximum(old, jnp.max(scores, axis=1, keepdims=True))
            w = jnp.where(allowed, jnp.exp(scores - new), 0.0).astype(BF)
            fade = jnp.exp(old - new)
            top_s[t] = new
            sum_s[t] = sum_s[t] * fade + jnp.sum(w.astype(F32), axis=1, keepdims=True)
            acc_s[t] = acc_s[t] * fade + jnp.dot(w, kv[cc, 1], preferred_element_type=F32)

        pl.loop(0, 4)(tile)

    pl.loop(0, c + 1)(key_block)

    def head_tile(t):
        out = (acc_s[t] / sum_s[t]).astype(BF)
        b1 = t // 2
        b0 = (b1 + t % 2) % 2
        for hd in range(2):
            for yy in range(4):
                at = hd * 128 + yy * 32
                h_ref[b1, b0, yy // 2, (yy // 2 + yy) % 2, :, :, hd * 128 : hd * 128 + 128] = out[at : at + 32].reshape(2, 16, 128)

    pl.loop(0, 4)(head_tile)

    def rs_index(f, s, bit):
        order = RS_ORDER[f]
        idx = [FULL] * 5
        for d in order[:s]:
            idx[d] = own5[d]
        idx[order[s]] = bit
        return tuple(idx)

    def rs_copy(buf, recv, ss, rs, f, s):
        d = RS_ORDER[f][s]
        return remote(
            buf.at[(f,) + rs_index(f, s, 1 - own5[d])], recv[s].at[f], ss.at[f, s], rs.at[f, s], rs_peer[d]
        )

    def rs_add(buf, recv, f, s, bit):
        order = RS_ORDER[f]
        step = order[s + 1]
        left = sorted(order[s + 2 :])
        n = len(left)

        def one(i):
            bits = dict(zip(left, block_bits(i, n)))
            bits[step] = bit
            idx = list(own5)
            for d in bits:
                idx[d] = bits[d]
            idx = (f,) + tuple(idx)
            got = recv[s][(f,) + tuple(bits[d] for d in sorted(bits))]
            buf[idx] = (buf[idx].astype(F32) + got.astype(F32)).astype(BF)

        if n:
            pl.loop(0, 2**n)(one)
        else:
            one(0)

    recv1 = (r10, r11, r12, r13, r14)
    recv2 = (r20, r21, r22, r23, r24)

    def project(f, bit):
        idx = rs_index(f, 0, bit)
        rows = h_ref[idx].reshape(256, 256)
        for t in range(2):
            cols = f * 1024 + t * 512
            out = jnp.dot(rows, ow_ref[:, cols : cols + 512], preferred_element_type=F32)
            p1[(f,) + idx + (FULL, slice(t * 512, t * 512 + 512))] = out.astype(BF).reshape(2, 2, 2, 2, 16, 512)

    first = []
    for f in range(4):
        project(f, 1 - own5[RS_ORDER[f][0]])
        cp = rs_copy(p1, recv1, s1s, s1r, f, 0)
        cp.start()
        first.append(cp)

    other = pl.ds(pl.multiple_of((1 - k) * HALF, HALF), HALF)
    mine = pl.ds(pl.multiple_of(k * HALF, HALF), HALF)
    own_rows = pl.ds(pl.multiple_of(c * FFS, FFS), FFS)

    def quarter(cc):
        return pl.ds(pl.multiple_of(cc * QUART, QUART), QUART)

    weight_copies = [
        remote(wg_ref.at[other], wgs, wss.at[0], wsr.at[0], sib),
        remote(wu_ref.at[other], wus, wss.at[1], wsr.at[1], sib),
        remote(wd_ref.at[:, quarter(zh * 2 + 1 - k)], wdq.at[own_rows], wss.at[2], wsr.at[2], sib),
        remote(wd_ref.at[:, quarter((1 - zh) * 2 + k)], wdq.at[own_rows], wss.at[3], wsr.at[3], far),
        remote(wd_ref.at[:, quarter((1 - zh) * 2 + 1 - k)], wdq.at[own_rows], wss.at[4], wsr.at[4], farsib),
    ]
    local_copies = [
        pltpu.make_async_copy(wg_ref.at[mine], wgk, lsem.at[0]),
        pltpu.make_async_copy(wu_ref.at[mine], wuk, lsem.at[1]),
        pltpu.make_async_copy(wd_ref.at[:, quarter(c)], wdq.at[own_rows], lsem.at[2]),
    ]
    for cp in weight_copies + local_copies:
        cp.start()

    for f in range(4):
        project(f, own5[RS_ORDER[f][0]])
    for j in range(2):

        @pl.when(zh == 0)
        def _():
            kv_copy(1, far, c, j).wait_send()
            kv_copy(2, farsib, c, j).wait_send()

        @pl.when(k == 0)
        def _():
            kv_copy(0, sib, c, j).wait_send()

    def finish_rs(buf, recv, ss, rs, wait_first):
        last = [None] * 4
        for s in range(4):
            for f in range(4):
                if s == 0:
                    wait_first(f)
                else:
                    last[f].wait()
                d = RS_ORDER[f][s + 1]
                rs_add(buf, recv, f, s, 1 - own5[d])
                last[f] = rs_copy(buf, recv, ss, rs, f, s + 1)
                last[f].start()
                rs_add(buf, recv, f, s, own5[d])
        out = []
        for f in range(4):
            last[f].wait()
            out.append(buf[(f,) + own5].astype(F32) + recv[4][f].astype(F32))
        return out

    parts = finish_rs(p1, recv1, s1s, s1r, lambda f: first[f].wait())

    squares = jnp.zeros((16, 1), F32)
    for f in range(4):
        cols = slice(f * 1024, f * 1024 + 1024)
        attn_ref[:, cols] = parts[f]
        st = (resid_ref[:, cols].astype(F32) + parts[f]).astype(BF)
        stream[:, cols] = st
        sf = st.astype(F32)
        squares = squares + jnp.sum(sf * sf, axis=1, keepdims=True)
    inv = lax.rsqrt(squares / D + 1e-06)
    for f in range(4):
        cols = slice(f * 1024, f * 1024 + 1024)
        out = (stream[:, cols].astype(F32) * inv * gain_ref[:, cols]).astype(BF)
        norm[f // 2, :, (f % 2) * 1024 : (f % 2) * 1024 + 1024] = out
    gates = gate_ref[...]
    top = gates.astype(BF)
    rest = gates - top.astype(F32)
    middle = rest.astype(BF)
    low = (rest - middle.astype(F32)).astype(BF)
    lane = lax.broadcasted_iota(jnp.int32, (16, 128), 1)
    gates = jnp.where(lane < EXPERTS, top.astype(F32), jnp.where(lane < 2 * EXPERTS, middle.astype(F32), low.astype(F32)))
    for i in range(2):
        norm[i, :, HALF:] = gates.astype(BF)

    xf = (x0, x1, x2, x3, x4, x5)
    swap = remote(norm.at[1 - k], csh, ccs.at[0], ccr.at[0], sib)
    swap.start()
    own_tok = pl.ds(pl.multiple_of(k * 16, 16), 16)
    sib_tok = pl.ds(pl.multiple_of((1 - k) * 16, 16), 16)
    for f in range(6):
        xf[f][own6 + (own_tok, slice(0, USED[f]))] = norm[k, :, OFFS[f] : OFFS[f] + USED[f]]
    x4[own6 + (own_tok, slice(256, 384))] = norm[k, :, HALF:]
    swap.wait()
    for f in range(6):
        xf[f][own6 + (sib_tok, slice(0, USED[f]))] = csh[:, OFFS[f] : OFFS[f] + USED[f]]
    x4[own6 + (sib_tok, slice(256, 384))] = csh[:, HALF:]

    def ag_copy(f, s, j):
        idx = list(own6)
        for t in range(j):
            idx[CYCLE[(f + t) % 6]] = FULL
        if j >= 0:
            d = CYCLE[(f + j) % 6]
            idx[d] = 1 - own6[d]
        part = xf[f].at[tuple(idx)]
        return remote(part, part, ags.at[f, s, j + 1], agr.at[f, s, j + 1], ag_peer[CYCLE[(f + s) % 6]])

    for s in range(6):
        for f in range(6):
            ag_copy(f, s, -1).start()
    for s in range(6):
        for f in range(6):
            for j in range(-1, s):
                ag_copy(f, s, j).wait_recv()
            for t in range(s + 1, 6):
                ag_copy(f, t, s).start()
    for s in range(6):
        for f in range(6):
            for j in range(-1, s):
                ag_copy(f, s, j).wait_send()

    for cp in weight_copies + local_copies:
        cp.wait()

    def chunk_bits(i):
        return (1 - own5[0] + i // 2) % 2, (1 - own5[1] + i % 2) % 2

    def chunk(i):
        b1, b0 = chunk_bits(i)
        return b1 * 2 + b0

    def chunk_rows(m):
        return pl.ds(pl.multiple_of(m * 256, 256), 256)

    def select(m):
        for g in range(2):
            pick = sel_ref[m * 2 + g]
            rows = pl.ds(pl.multiple_of(m * 256 + g * 128, 128), 128)
            for f in range(6):
                block = xf[f][m // 2, m % 2, g].reshape(256, WIDTHS[f])[:, : USED[f]]
                xs[rows, OFFS[f] : OFFS[f] + USED[f]] = jnp.dot(pick, block, preferred_element_type=F32).astype(BF)

    def partial_copy(m):
        return remote(psend.at[m], precv.at[m], pss.at[m], psr.at[m], sib)

    def other_units(m):
        a = xs[chunk_rows(m), :]
        psend[m, :, :FFS] = jnp.dot(a, wgs[...], preferred_element_type=F32).astype(BF)
        psend[m, :, FFS:] = jnp.dot(a, wus[...], preferred_element_type=F32).astype(BF)
        partial_copy(m).start()

    def hidden_cols(cc):
        return pl.ds(pl.multiple_of(cc * FFS, 128), FFS)

    def hidden_copy(m, cc, kind, to):
        part = hall.at[chunk_rows(m), hidden_cols(cc)]
        return remote(part, part, hss.at[kind, m], hsr.at[kind, m], to)

    def own_units(m):
        a = xs[chunk_rows(m), :]
        gate = jnp.dot(a, wgk[...], preferred_element_type=F32)
        upper = jnp.dot(a, wuk[...], preferred_element_type=F32)
        partial_copy(m).wait()
        gate = gate + precv[m, :, :FFS].astype(F32)
        upper = upper + precv[m, :, FFS:].astype(F32)
        hall[chunk_rows(m), hidden_cols(c)] = (gate / (1.0 + jnp.exp(-gate)) * upper).astype(BF)
        hidden_copy(m, c, 0, far).start()
        hidden_copy(m, c, 1, sib).start()

    def units(i):
        @pl.when(i < 4)
        def _():
            m = chunk(i)
            select(m)
            other_units(m)

        @pl.when(i > 0)
        def _():
            own_units(chunk(i - 1))

    pl.loop(0, 5)(units)
    far_c = (1 - zh) * 2 + k

    def half_copy(f, b1, b0):
        if f == 0:
            src, dst, sem = p2.at[0, b1, b0], r20.at[0, b0], b0
        elif f == 2:
            src, dst, sem = p2.at[2, b1, b0], r20.at[2, b1], b1
        elif f == 1:
            src, dst, sem = p2.at[1, b1, b0, 1 - own5[2]], r20.at[1, b1, b0], b1 * 2 + b0
        else:
            src, dst, sem = p2.at[3, b1, b0, :, 1 - own5[3]], r20.at[3, b1, b0], b1 * 2 + b0
        return remote(src, dst, has.at[f, sem], har.at[f, sem], rs_peer[RS_ORDER[f][0]])

    lane = lax.broadcasted_iota(jnp.int32, (256, 128), 1)
    my_lanes = jnp.logical_or(lane == e, jnp.logical_or(lane == e + EXPERTS, lane == e + 2 * EXPERTS))

    def down(i):
        b1, b0 = chunk_bits(i)
        m = b1 * 2 + b0
        hidden_copy(m, c, 1, sib).wait()
        hidden_copy(m, far_c, 2, sib).wait()
        a = hall[chunk_rows(m), :]
        weights = []
        for g in range(2):
            block = x4[b1, b0, g].reshape(256, 384)[:, 256:].astype(F32)
            weights.append(jnp.sum(jnp.where(my_lanes, block, 0.0), axis=1, keepdims=True))
        for f in range(4):
            cols = slice(f * 256, f * 256 + 256)
            out = jnp.dot(a, wdq[:, cols], preferred_element_type=F32).astype(BF)
            for g in range(2):
                tok = lax.dot_general(
                    sel_ref[m * 2 + g], out[g * 128 : g * 128 + 128], (((0,), (0,)), ((), ())),
                    preferred_element_type=F32,
                )
                tok = (tok * weights[g]).astype(BF)
                for yb in range(2):
                    for j in range(4):
                        zlo, zhi = ZMAP[j]
                        at = (yb * 4 + j) * 32
                        p2[f, b1, b0, g, yb, zlo, zhi * 32 : zhi * 32 + 32, :] = tok[at : at + 32]
            if f == 0:
                pl.when(i < 2)(lambda: half_copy(0, b1, b0).start())
            elif f == 2:
                pl.when(i % 2 == 0)(lambda: half_copy(2, b1, b0).start())
            else:
                half_copy(f, b1, b0).start()

    def spread(i):
        @pl.when(i < 4)
        def _():
            m = chunk(i)
            hidden_copy(m, c, 0, far).wait()
            hidden_copy(m, far_c, 2, sib).start()

        @pl.when(i > 0)
        def _():
            down(i - 1)

    pl.loop(0, 5)(spread)

    def wait_half(f):
        for b in range(2 if f % 2 == 0 else 4):
            if f == 0:
                half_copy(0, 1 - own5[0], b).wait()
            elif f == 2:
                half_copy(2, b, 1 - own5[1]).wait()
            else:
                half_copy(f, b // 2, b % 2).wait()

    def gram(j):
        cols = pl.ds(pl.multiple_of(j * 256, 256), 256)
        gram_ref[:, cols] = lax.dot_general(
            hall[:, hidden_cols(c)], hall[:, cols], (((0,), (0,)), ((), ())), preferred_element_type=F32
        )

    pl.loop(0, 6)(gram)

    parts = finish_rs(p2, recv2, s2s, s2r, wait_half)
    for f in range(4):
        cols = slice(f * 256, f * 256 + 256)
        fsend[:, :, cols] = parts[f].astype(BF).reshape(4, 16, 256)
    final = []
    for i, (cc, to) in enumerate(
        ((zh * 2 + 1 - k, sib), ((1 - zh) * 2 + k, far), ((1 - zh) * 2 + 1 - k, farsib))
    ):
        cp = remote(fsend.at[cc], frecv.at[c], fss.at[i], fsr.at[i], to)
        cp.start()
        final.append(cp)
    frecv[c] = fsend[c]
    for cp in final:
        cp.wait()
    for cc in range(4):
        cols = slice(cc * QUART, cc * QUART + QUART)
        mixed_ref[:, cols] = (stream[:, cols].astype(F32) + frecv[cc].astype(F32)).astype(BF)


def fused(q, ow, resid, gain, gate, rank, keys, values, wg, wu, wd):
    dma = pltpu.SemaphoreType.DMA
    vm = pl.BlockSpec(memory_space=pltpu.VMEM)
    hbm = pl.BlockSpec(memory_space=pl.ANY)
    two = (2,) * 6

    def rs_scratch(rows, cols):
        out = [pltpu.VMEM((4,) + (2,) * 5 + (rows, cols), BF)]
        for s in range(5):
            out.append(pltpu.VMEM((4,) + (2,) * (4 - s) + (rows, cols), BF))
        return out

    scratch = (
        [pltpu.VMEM((4, 2, 512, HEAD_SIZE), BF), pltpu.VMEM((4, 256, 1), F32), pltpu.VMEM((4, 256, 1), F32)]
        + [pltpu.VMEM((4, 256, HEAD_SIZE), F32), pltpu.VMEM((2,) * 5 + (16, 256), BF), pltpu.VMEM((8, 128, 256), BF)]
        + rs_scratch(16, 1024)
        + [pltpu.VMEM((2, 16, WIDE), BF), pltpu.VMEM((16, D), BF), pltpu.VMEM((16, WIDE), BF)]
        + [pltpu.VMEM(two + (32, w), BF) for w in WIDTHS]
        + [pltpu.VMEM((HALF, FFS), BF)] * 4
        + [pltpu.VMEM((FF, QUART), BF), pltpu.VMEM((1024, HALF), BF)]
        + [pltpu.VMEM((4, 256, 2 * FFS), BF)] * 2
        + [pltpu.VMEM((1024, FF), BF)]
        + rs_scratch(64, 256)
        + [pltpu.VMEM((4, 16, QUART), BF)] * 2
        + [dma((2,)), dma((3, 2)), dma((4, 2))]
        + [dma((4, 5)), dma((4, 5)), dma((5,)), dma((5,)), dma((3,)), dma((1,)), dma((1,))]
        + [dma((6, 6, 6)), dma((6, 6, 6)), dma((4,)), dma((4,)), dma((3, 4)), dma((3, 4))]
        + [dma((4, 4)), dma((4, 4)), dma((4, 5)), dma((4, 5)), dma((3,)), dma((3,))]
    )
    return pl.pallas_call(
        kernel,
        out_shape=(
            jax.ShapeDtypeStruct((16, D), BF),
            jax.ShapeDtypeStruct((16, D), F32),
            jax.ShapeDtypeStruct((FFS, FF), F32),
        ),
        in_specs=[vm] * 6 + [hbm] * 5,
        out_specs=(vm, vm, vm),
        scratch_shapes=scratch,
        compiler_params=pltpu.CompilerParams(
            collective_id=0, has_side_effects=True, vmem_limit_bytes=62 * 2**20
        ),
        name="layer",
    )(q, ow, resid, gain, gate, rank, keys, values, wg, wu, wd)


def gray(a, axis):
    parts = [lax.slice_in_dim(a, i, i + 1, axis=axis) for i in GRAY]
    return jnp.concatenate(parts, axis=axis)


def gathered_order(a):
    rest = a.shape[1:]
    n = len(rest)
    a = a.reshape((2, 2, 4, 4, 2, 16) + rest)
    a = jnp.transpose(a, (2, 3, 0, 4, 1, 5) + tuple(range(6, 6 + n)))
    a = a.reshape((4, 4, 4, 32) + rest)
    for axis in range(3):
        a = gray(a, axis)
    return a.reshape((2048,) + rest)


def local(
    resid, query, keys, values, out_weight, post_gain, route_idx, gates, w_gate, w_up, w_down
):
    exp_pos = lax.axis_index("exp")
    block = lax.axis_index("ctx") * EXPERTS + exp_pos
    own_idx = lax.dynamic_slice_in_dim(route_idx, block * 16, 16, 0)
    expert = jnp.arange(128, dtype=jnp.int32)
    expert = jnp.where(expert < 3 * EXPERTS, expert % EXPERTS, -1)
    gate = jnp.sum(jnp.where(own_idx[:, :, None] == expert[None, None, :], gates[:, :, None], 0.0), axis=1)
    member = jnp.any(route_idx == exp_pos, axis=1)
    count = jnp.sum(member.astype(F32))
    member = gathered_order(member.astype(BF)).reshape(128, 16)
    before = (jnp.arange(16)[:, None] < jnp.arange(16)[None, :]).astype(BF)
    rank = jnp.dot(member, before, preferred_element_type=F32)
    rank = jnp.where(member > 0, rank, -1.0).astype(jnp.int32).reshape(8, 1, 256)
    mixed, attn_out, gram = fused(
        query, out_weight, resid, post_gain.reshape(1, D), gate, rank, keys, values, w_gate[0], w_up[0], w_down[0]
    )
    return (mixed, attn_out, (gram / count)[None])


def solution(mesh):
    placed = (
        P(("ctx", "exp"), None),
        P("ctx", "exp"),
        P("ctx", None),
        P("ctx", None),
        P("exp", None),
        P(),
        P(),
        P(("ctx", "exp"), None),
        P("exp", None, "ctx"),
        P("exp", None, "ctx"),
        P("exp", "ctx", None),
    )
    return jax.shard_map(
        local,
        mesh=mesh,
        in_specs=placed,
        out_specs=(P(("ctx", "exp"), None), P(("ctx", "exp"), None), P("exp", "ctx", None)),
        check_vma=False,
    )
```

```python
import functools
import math

import jax
import jax.numpy as jnp
from jax import lax
from jax.experimental import pallas as pl
from jax.experimental.pallas import tpu as pltpu
from jax.sharding import PartitionSpec as P

EXPERTS = 32
HEAD_SIZE = 128
D = 4096
FF = 1536
FFS = 384
HALF = D // 2
QUART = D // 4
MESH = pl.DeviceIdType.MESH
BF = jnp.bfloat16
F32 = jnp.float32

RS_ORDER = ((0, 2, 1, 3, 4), (2, 1, 3, 0, 4), (1, 3, 0, 2, 4), (3, 0, 2, 1, 4))
CYCLE = (0, 2, 4, 1, 3, 5)
WIDTHS = (384, 384, 384, 384, 384, 256)
USED = (384, 384, 384, 384, 256, 256)
OFFS = (0, 384, 768, 1152, 1536, 1792)
WIDE = HALF + 128
GRAY = (0, 1, 3, 2)
ZMAP = ((0, 0), (1, 0), (1, 1), (0, 1))
FULL = slice(None)


def block_bits(i, n):
    return [(i // (2 ** (n - 1 - j))) % 2 for j in range(n)]


def kernel(
    q_hbm, ow_hbm, resid_hbm, gain_hbm, gate_hbm, rank_hbm, keys_ref, values_ref, wg_ref, wu_ref, wd_ref,
    mixed_hbm, attn_hbm, gram_hbm,
    q_ref, resid_ref, gain_ref, gate_ref, rank_ref, mixed_ref, attn_ref, gram_ref, isem, osem,
    kk, vv, top_s, acc_s, h_ref, sel_ref, ow_ref,
    p1, r10, r11, r12, r13, norm, stream, csh, x0, x1, x2, x3, x4, x5,
    wgk, wuk, wgs, wus, wdq, xs, psend, precv, hall, p2, r20, r21, r22, r23, frecv,
    kvl, kvs, kvr,
    s1s, s1r, t1s, t1r, wss, wsr, lsem, ccs, ccr, ags, agr, pss, psr, hss, hsr, has, har, s2s, s2r, fss, fsr,
):
    c = lax.axis_index("ctx")
    e = lax.axis_index("exp")
    x, y, zl, zh, k = e // 8, (e // 2) % 4, e % 2, c // 2, c % 2

    def dev(x_, y_, zl_, zh_, k_):
        return (zh_ * 2 + k_, x_ * 8 + y_ * 2 + zl_)

    def flip1(v):
        return v + 1 - 2 * (v % 2)

    peer_x = (dev(3 - x, y, zl, zh, k), dev(flip1(x), y, zl, zh, k))
    peer_y = (dev(x, 3 - y, zl, zh, k), dev(x, flip1(y), zl, zh, k))
    peer_z1 = dev(x, y, 1 - zl, zh, k)
    peer_z3 = dev(x, y, 1 - zl, 1 - zh, k)
    sib = dev(x, y, zl, zh, 1 - k)
    far = dev(x, y, zl, 1 - zh, k)
    farsib = dev(x, y, zl, 1 - zh, 1 - k)
    rs_peer = (peer_x[0], peer_x[1], peer_y[0], peer_y[1], peer_z1)
    diagonal = (
        dev(3 - x, y, 1 - zl, zh, k), dev(flip1(x), y, 1 - zl, zh, k),
        dev(x, 3 - y, 1 - zl, zh, k), dev(x, flip1(y), 1 - zl, zh, k),
    )
    z1sib, z3sib = dev(x, y, 1 - zl, zh, 1 - k), dev(x, y, 1 - zl, 1 - zh, 1 - k)
    ag_peer = (peer_x[0], peer_x[1], peer_y[0], peer_y[1], peer_z3, peer_z1)
    xb1, yb1 = x // 2, y // 2
    own5 = (xb1, (xb1 + x % 2) % 2, yb1, (yb1 + y % 2) % 2, zl)
    own6 = own5[:4] + (zh, (zh + zl) % 2)

    hbm_vmem = (
        (q_hbm, q_ref), (rank_hbm, rank_ref), (ow_hbm, ow_ref), (resid_hbm, resid_ref), (gain_hbm, gain_ref),
        (gate_hbm, gate_ref),
    )
    input_copies = [pltpu.make_async_copy(a, b, isem.at[i]) for i, (a, b) in enumerate(hbm_vmem)]
    attn_copy = pltpu.make_async_copy(attn_ref, attn_hbm, osem.at[0])
    gram_copy = pltpu.make_async_copy(gram_ref, gram_hbm, osem.at[1])
    mixed_copy = pltpu.make_async_copy(mixed_ref, mixed_hbm, osem.at[2])
    barrier = pltpu.get_barrier_semaphore()
    partners = list(ag_peer) + [sib, far, farsib, z1sib, z3sib] + list(diagonal)
    for p in partners:
        pl.semaphore_signal(barrier, inc=1, device_id=p, device_id_type=MESH)
    pl.semaphore_wait(barrier, len(partners))

    def remote(src, dst, ss, rs, to):
        return pltpu.make_async_remote_copy(
            src_ref=src, dst_ref=dst, send_sem=ss, recv_sem=rs, device_id=to, device_id_type=MESH
        )

    head_cols = pl.ds(pl.multiple_of(x * HEAD_SIZE, HEAD_SIZE), HEAD_SIZE)
    kv_src = (keys_ref.at[:, head_cols], values_ref.at[:, head_cols])

    def kv_dst(cc, j):
        return vv.at[cc, :, 0:HEAD_SIZE] if j else kk.at[cc]

    def kv_copy(i, to, cc, j):
        return remote(kv_src[j], kv_dst(cc, j), kvs.at[i, j], kvr.at[cc, j], to)

    def kv_local(j):
        return pltpu.make_async_copy(kv_src[j], kv_dst(c, j), kvl.at[j])

    def kv_forward(j):
        return remote(kv_dst(k, j), kv_dst(k, j), kvs.at[2, j], kvr.at[k, j], sib)

    for j in range(2):

        @pl.when(zh == 0)
        def _():
            kv_copy(1, peer_z3, c, j).start()

    for j in range(2):

        @pl.when(k == 0)
        def _():
            kv_copy(0, sib, c, j).start()

        kv_local(j).start()

    for cp in input_copies:
        cp.start()

    other = pl.ds(pl.multiple_of((1 - k) * HALF, HALF), HALF)
    mine = pl.ds(pl.multiple_of(k * HALF, HALF), HALF)
    own_rows = pl.ds(pl.multiple_of(c * FFS, FFS), FFS)

    def quarter(cc):
        return pl.ds(pl.multiple_of(cc * QUART, QUART), QUART)

    near_copies = [
        remote(wg_ref.at[other], wgs, wss.at[0], wsr.at[0], sib),
        remote(wu_ref.at[other], wus, wss.at[1], wsr.at[1], sib),
        remote(wd_ref.at[:, quarter(zh * 2 + 1 - k)], wdq.at[own_rows], wss.at[2], wsr.at[2], sib),
        pltpu.make_async_copy(wg_ref.at[mine], wgk, lsem.at[0]),
        pltpu.make_async_copy(wu_ref.at[mine], wuk, lsem.at[1]),
        pltpu.make_async_copy(wd_ref.at[:, quarter(c)], wdq.at[own_rows], lsem.at[2]),
    ]
    far_copies = [
        remote(wd_ref.at[:, quarter((1 - zh) * 2 + k)], wdq.at[own_rows], wss.at[3], wsr.at[3], far),
        remote(wd_ref.at[:, quarter((1 - zh) * 2 + 1 - k)], wdq.at[own_rows], wss.at[4], wsr.at[4], farsib),
    ]

    @pl.when(zh == 1)
    def _():
        for cp in far_copies:
            cp.start()

    slot = lax.broadcasted_iota(jnp.int32, (128, 256), 0)
    token = lax.broadcasted_iota(jnp.int32, (128, 256), 1)
    place = jnp.where(slot // 8 == token // 16, slot % 8, -2)

    for cp in input_copies[:2]:
        cp.wait()

    def pick_slots(g):
        sel_ref[g] = jnp.where(place == rank_ref[g], 1.0, 0.0).astype(BF)

    pl.loop(0, 8)(pick_slots)
    for cc in range(4):
        vv[cc, :, HEAD_SIZE:] = jnp.ones((512, HEAD_SIZE), BF)
    scale = math.log2(math.e) / math.sqrt(HEAD_SIZE)
    trans = (((1,), (1,)), ((), ()))

    def queries(t):
        rows = slice(t * 128, t * 128 + 128)
        return jnp.concatenate([q_ref[rows, :HEAD_SIZE], q_ref[rows, HEAD_SIZE:]], axis=0)

    for j in range(2):
        kv_local(j).wait()
    for cp in near_copies:
        cp.start()
    for t in range(4):
        n = t * 128 + 128
        scores = lax.dot_general(queries(t), kk[c, :n], trans, preferred_element_type=F32)
        q_place = lax.rem(lax.broadcasted_iota(jnp.int32, (256, n), 0), 128) + t * 128
        scores = jnp.where(q_place >= lax.broadcasted_iota(jnp.int32, (256, n), 1), scores, -1e30)
        new = jnp.max(scores, axis=1, keepdims=True)
        w = jnp.exp2((scores - new) * scale).astype(BF)
        top_s[t] = new
        acc_s[t] = jnp.dot(w, vv[c, :n], preferred_element_type=F32)

    @pl.when(zh == 1)
    def _():
        for j in range(2):
            kv_copy(1, peer_z3, k, j).wait_recv()
            kv_forward(j).start()

    def key_block(i):
        cc = c - i

        @pl.when(jnp.logical_or(zh == 0, cc != k))
        def _():
            for j in range(2):
                kv_copy(0, sib, cc, j).wait_recv()

        for t in range(4):
            scores = lax.dot_general(queries(t), kk[cc], trans, preferred_element_type=F32)
            old = top_s[t]
            new = jnp.maximum(old, jnp.max(scores, axis=1, keepdims=True))
            w = jnp.exp2((scores - new) * scale).astype(BF)
            fade = jnp.exp2((old - new) * scale)
            top_s[t] = new
            acc_s[t] = acc_s[t] * fade + jnp.dot(w, vv[cc], preferred_element_type=F32)

    pl.loop(1, c + 1)(key_block)

    @pl.when(zh == 0)
    def _():
        for cp in far_copies:
            cp.start()

    def head_tile(t):
        out = (acc_s[t, :, :HEAD_SIZE] / acc_s[t, :, HEAD_SIZE:]).astype(BF)
        b1 = t // 2
        b0 = (b1 + t % 2) % 2
        for hd in range(2):
            for yy in range(4):
                at = hd * 128 + yy * 32
                h_ref[b1, b0, yy // 2, (yy // 2 + yy) % 2, :, :, hd * 128 : hd * 128 + 128] = out[at : at + 32].reshape(2, 16, 128)

    pl.loop(0, 4)(head_tile)

    def rs_index(f, s, bit):
        order = RS_ORDER[f]
        idx = [FULL] * 5
        for d in order[:s]:
            idx[d] = own5[d]
        idx[order[s]] = bit
        return tuple(idx)

    def rs_copy(buf, recv, ss, rs, f, s):
        d = RS_ORDER[f][s]
        return remote(
            buf.at[(f,) + rs_index(f, s, 1 - own5[d])], recv[s].at[f], ss.at[f, s], rs.at[f, s], rs_peer[d]
        )

    def rs_add(buf, recv, f, s, bit):
        order = RS_ORDER[f]
        step = order[s + 1]
        left = sorted(order[s + 2 :])
        n = len(left)

        def one(i):
            bits = dict(zip(left, block_bits(i, n)))
            bits[step] = bit
            idx = list(own5)
            for d in bits:
                idx[d] = bits[d]
            idx = (f,) + tuple(idx)
            got = recv[s][(f,) + tuple(bits[d] for d in sorted(bits))]
            buf[idx] = (buf[idx].astype(F32) + got.astype(F32)).astype(BF)

        if n:
            pl.loop(0, 2**n)(one)
        else:
            one(0)

    recv1 = (r10, r11, r12)
    recv2 = (r20, r21, r22, r23)

    def project(f, bit):
        idx = rs_index(f, 0, bit)
        rows = h_ref[idx].reshape(256, 256)
        for t in range(2):
            cols = f * 1024 + t * 512
            out = jnp.dot(rows, ow_ref[:, cols : cols + 512], preferred_element_type=F32)
            p1[(f,) + idx + (FULL, slice(t * 512, t * 512 + 512))] = out.astype(BF).reshape(2, 2, 2, 2, 16, 512)

    for cp in input_copies[2:]:
        cp.wait()
    first = []
    for f in range(4):
        project(f, 1 - own5[RS_ORDER[f][0]])
        cp = rs_copy(p1, recv1, s1s, s1r, f, 0)
        cp.start()
        first.append(cp)

    for f in range(4):
        project(f, own5[RS_ORDER[f][0]])
    for j in range(2):

        @pl.when(zh == 0)
        def _():
            kv_copy(1, peer_z3, c, j).wait_send()

        @pl.when(zh == 1)
        def _():
            kv_forward(j).wait_send()

        @pl.when(k == 0)
        def _():
            kv_copy(0, sib, c, j).wait_send()

    def run_rs(buf, recv, ss, rs, wait_first, steps, tail):
        last = [None] * 4
        for s in range(steps):
            for f in range(4):
                if s == 0:
                    wait_first(f)
                else:
                    last[f].wait()
                d = RS_ORDER[f][s + 1]
                rs_add(buf, recv, f, s, 1 - own5[d])
                if s + 1 < steps:
                    last[f] = rs_copy(buf, recv, ss, rs, f, s + 1)
                    last[f].start()
                rs_add(buf, recv, f, s, own5[d])
                if s + 1 == steps:
                    tail(f)

    tails = []

    def direct(f):
        d = RS_ORDER[f][3]
        for i, (to, flips) in enumerate(((rs_peer[d], (d,)), (peer_z1, (4,)), (diagonal[d], (d, 4)))):
            idx = tuple(1 - own5[j] if j in flips else own5[j] for j in range(5))
            cp = remote(p1.at[(f,) + idx], r13.at[f, i], t1s.at[f, i], t1r.at[f, i], to)
            cp.start()
            tails.append(cp)

    run_rs(p1, recv1, s1s, s1r, lambda f: first[f].wait(), 3, direct)
    parts = []
    for f in range(4):
        for i in range(3):
            tails[f * 3 + i].wait()
        got = [r13[f, i].astype(F32) for i in range(3)]
        parts.append((p1[(f,) + own5].astype(F32) + got[0]) + (got[1] + got[2]))

    squares = jnp.zeros((16, 1), F32)
    for f in range(4):
        cols = slice(f * 1024, f * 1024 + 1024)
        attn_ref[:, cols] = parts[f]
        st = (resid_ref[:, cols].astype(F32) + parts[f]).astype(BF)
        stream[:, cols] = st
        sf = st.astype(F32)
        squares = squares + jnp.sum(sf * sf, axis=1, keepdims=True)
    attn_copy.start()
    inv = lax.rsqrt(squares / D + 1e-06)
    for f in range(4):
        cols = slice(f * 1024, f * 1024 + 1024)
        out = (stream[:, cols].astype(F32) * inv * gain_ref[:, cols]).astype(BF)
        norm[f // 2, :, (f % 2) * 1024 : (f % 2) * 1024 + 1024] = out
    gates = gate_ref[...]
    top = gates.astype(BF)
    rest = gates - top.astype(F32)
    middle = rest.astype(BF)
    low = (rest - middle.astype(F32)).astype(BF)
    lane = lax.broadcasted_iota(jnp.int32, (16, 128), 1)
    gates = jnp.where(lane < EXPERTS, top.astype(F32), jnp.where(lane < 2 * EXPERTS, middle.astype(F32), low.astype(F32)))
    for i in range(2):
        norm[i, :, HALF:] = gates.astype(BF)

    xf = (x0, x1, x2, x3, x4, x5)
    swap = remote(norm.at[1 - k], csh, ccs.at[0], ccr.at[0], sib)
    swap.start()
    own_tok = pl.ds(pl.multiple_of(k * 16, 16), 16)
    sib_tok = pl.ds(pl.multiple_of((1 - k) * 16, 16), 16)
    for f in range(6):
        xf[f][own6 + (own_tok, slice(0, USED[f]))] = norm[k, :, OFFS[f] : OFFS[f] + USED[f]]
    x4[own6 + (own_tok, slice(256, 384))] = norm[k, :, HALF:]
    swap.wait()
    for f in range(6):
        xf[f][own6 + (sib_tok, slice(0, USED[f]))] = csh[:, OFFS[f] : OFFS[f] + USED[f]]
    x4[own6 + (sib_tok, slice(256, 384))] = csh[:, HALF:]

    def ag_copy(f, s, j):
        idx = list(own6)
        for t in range(j):
            idx[CYCLE[(f + t) % 6]] = FULL
        if j >= 0:
            d = CYCLE[(f + j) % 6]
            idx[d] = 1 - own6[d]
        part = xf[f].at[tuple(idx)]
        return remote(part, part, ags.at[f, s, j + 1], agr.at[f, s, j + 1], ag_peer[CYCLE[(f + s) % 6]])

    for s in range(6):
        for f in range(6):
            ag_copy(f, s, -1).start()
    for s in range(6):
        for f in range(6):
            for j in range(-1, s):
                ag_copy(f, s, j).wait_recv()
            for t in range(s + 1, 6):
                ag_copy(f, t, s).start()
    for s in range(6):
        for f in range(6):
            for j in range(-1, s):
                ag_copy(f, s, j).wait_send()

    for cp in near_copies + far_copies:
        cp.wait()

    def chunk_bits(i):
        return (1 - own5[0] + i // 2) % 2, (1 - own5[1] + i % 2) % 2

    def chunk(i):
        b1, b0 = chunk_bits(i)
        return b1 * 2 + b0

    def chunk_rows(m):
        return pl.ds(pl.multiple_of(m * 256, 256), 256)

    def select(m):
        for g in range(2):
            pick = sel_ref[m * 2 + g]
            rows = pl.ds(pl.multiple_of(m * 256 + g * 128, 128), 128)
            for f in range(6):
                block = xf[f][m // 2, m % 2, g].reshape(256, WIDTHS[f])[:, : USED[f]]
                xs[rows, OFFS[f] : OFFS[f] + USED[f]] = jnp.dot(pick, block, preferred_element_type=F32).astype(BF)

    def partial_copy(m):
        return remote(psend.at[m], precv.at[m], pss.at[m], psr.at[m], sib)

    def other_units(m):
        a = xs[chunk_rows(m), :]
        psend[m, :, :FFS] = jnp.dot(a, wgs[...], preferred_element_type=F32).astype(BF)
        psend[m, :, FFS:] = jnp.dot(a, wus[...], preferred_element_type=F32).astype(BF)
        partial_copy(m).start()

    def hidden_cols(cc):
        return pl.ds(pl.multiple_of(cc * FFS, 128), FFS)

    def hidden_copy(m, cc, kind, to):
        part = hall.at[chunk_rows(m), hidden_cols(cc)]
        return remote(part, part, hss.at[kind, m], hsr.at[kind, m], to)

    def own_units(m):
        a = xs[chunk_rows(m), :]
        gate = jnp.dot(a, wgk[...], preferred_element_type=F32)
        upper = jnp.dot(a, wuk[...], preferred_element_type=F32)
        partial_copy(m).wait()
        gate = gate + precv[m, :, :FFS].astype(F32)
        upper = upper + precv[m, :, FFS:].astype(F32)
        hall[chunk_rows(m), hidden_cols(c)] = (gate / (1.0 + jnp.exp(-gate)) * upper).astype(BF)
        hidden_copy(m, c, 0, far).start()
        hidden_copy(m, c, 1, sib).start()

    def units(i):
        m = chunk(i)
        select(m)
        other_units(m)
        own_units(m)

    pl.loop(0, 4)(units)
    far_c = (1 - zh) * 2 + k

    def half_copy(f, b1, b0):
        if f == 0:
            src, dst, sem = p2.at[0, b1, b0], r20.at[0, b0], b0
        elif f == 2:
            src, dst, sem = p2.at[2, b1, b0], r20.at[2, b1], b1
        elif f == 1:
            src, dst, sem = p2.at[1, b1, b0, 1 - own5[2]], r20.at[1, b1, b0], b1 * 2 + b0
        else:
            src, dst, sem = p2.at[3, b1, b0, :, 1 - own5[3]], r20.at[3, b1, b0], b1 * 2 + b0
        return remote(src, dst, has.at[f, sem], har.at[f, sem], rs_peer[RS_ORDER[f][0]])

    lane = lax.broadcasted_iota(jnp.int32, (256, 128), 1)
    my_lanes = jnp.logical_or(lane == e, jnp.logical_or(lane == e + EXPERTS, lane == e + 2 * EXPERTS))

    def down(i):
        b1, b0 = chunk_bits(i)
        m = b1 * 2 + b0
        hidden_copy(m, c, 1, sib).wait()
        hidden_copy(m, far_c, 2, sib).wait()
        a = hall[chunk_rows(m), :]
        weights = []
        for g in range(2):
            block = x4[b1, b0, g].reshape(256, 384)[:, 256:].astype(F32)
            weights.append(jnp.sum(jnp.where(my_lanes, block, 0.0), axis=1, keepdims=True))
        for f in range(4):
            cols = slice(f * 256, f * 256 + 256)
            out = jnp.dot(a, wdq[:, cols], preferred_element_type=F32).astype(BF)
            for g in range(2):
                tok = lax.dot_general(
                    sel_ref[m * 2 + g], out[g * 128 : g * 128 + 128], (((0,), (0,)), ((), ())),
                    preferred_element_type=F32,
                )
                tok = (tok * weights[g]).astype(BF)
                for yb in range(2):
                    for j in range(4):
                        zlo, zhi = ZMAP[j]
                        at = (yb * 4 + j) * 32
                        p2[f, b1, b0, g, yb, zlo, zhi * 32 : zhi * 32 + 32, :] = tok[at : at + 32]
            if f == 0:
                pl.when(i < 2)(lambda: half_copy(0, b1, b0).start())
            elif f == 2:
                pl.when(i % 2 == 0)(lambda: half_copy(2, b1, b0).start())
            else:
                half_copy(f, b1, b0).start()

    def spread(i):
        @pl.when(i < 4)
        def _():
            m = chunk(i)
            hidden_copy(m, c, 0, far).wait()
            hidden_copy(m, far_c, 2, sib).start()

        @pl.when(i > 0)
        def _():
            down(i - 1)

    pl.loop(0, 5)(spread)

    def wait_half(f):
        for b in range(2 if f % 2 == 0 else 4):
            if f == 0:
                half_copy(0, 1 - own5[0], b).wait()
            elif f == 2:
                half_copy(2, b, 1 - own5[1]).wait()
            else:
                half_copy(f, b // 2, b % 2).wait()

    count = jnp.sum(jnp.where(rank_ref[:, 0, :] >= 0, 1.0, 0.0))

    def gram(j):
        cols = pl.ds(pl.multiple_of(j * 256, 256), 256)
        out = lax.dot_general(
            hall[:, hidden_cols(c)], hall[:, cols], (((0,), (0,)), ((), ())), preferred_element_type=F32
        )
        gram_ref[:, cols] = out / count

    pl.loop(0, 6)(gram)
    gram_copy.start()

    def nothing(f):
        return None

    run_rs(p2, recv2, s2s, s2r, wait_half, 4, nothing)
    final = []
    for i, (to, (flip_l, flip_h, flip_k)) in enumerate(
        (
            (sib, (0, 0, 1)), (peer_z1, (1, 0, 0)), (far, (0, 1, 0)), (peer_z3, (1, 1, 0)),
            (z1sib, (1, 0, 1)), (farsib, (0, 1, 1)), (z3sib, (1, 1, 1)),
        )
    ):
        to_l = 1 - zl if flip_l else zl
        to_c = (1 - zh if flip_h else zh) * 2 + (1 - k if flip_k else k)
        rows = pl.ds(pl.multiple_of(to_c * 16, 16), 16)
        cp = remote(p2.at[(FULL,) + own5[:4] + (to_l, rows)], frecv.at[zl, c], fss.at[i], fsr.at[i], to)
        cp.start()
        final.append(cp)
    rows = pl.ds(pl.multiple_of(c * 16, 16), 16)
    frecv[zl, c] = p2[(FULL,) + own5 + (rows,)]
    for cp in final:
        cp.wait()
    for cc in range(4):
        for f in range(4):
            cols = slice(cc * QUART + f * 256, cc * QUART + f * 256 + 256)
            routed = frecv[0, cc, f].astype(F32) + frecv[1, cc, f].astype(F32)
            mixed_ref[:, cols] = (stream[:, cols].astype(F32) + routed).astype(BF)
    mixed_copy.start()
    attn_copy.wait()
    gram_copy.wait()
    mixed_copy.wait()


def fused(q, ow, resid, gain, gate, rank, keys, values, wg, wu, wd):
    dma = pltpu.SemaphoreType.DMA
    hbm = pl.BlockSpec(memory_space=pl.ANY)
    two = (2,) * 6

    def rs_scratch(rows, cols, steps):
        out = [pltpu.VMEM((4,) + (2,) * 5 + (rows, cols), BF)]
        for s in range(steps):
            out.append(pltpu.VMEM((4,) + (2,) * (4 - s) + (rows, cols), BF))
        return out

    scratch = (
        [pltpu.VMEM((512, 256), BF), pltpu.VMEM((16, D), BF), pltpu.VMEM((1, D), F32), pltpu.VMEM((16, 128), F32)]
        + [pltpu.VMEM((8, 1, 256), jnp.int32), pltpu.VMEM((16, D), BF), pltpu.VMEM((16, D), F32)]
        + [pltpu.VMEM((FFS, FF), F32), dma((6,)), dma((3,))]
        + [pltpu.VMEM((4, 512, HEAD_SIZE), BF), pltpu.VMEM((4, 512, 2 * HEAD_SIZE), BF), pltpu.VMEM((4, 256, 1), F32)]
        + [pltpu.VMEM((4, 256, 2 * HEAD_SIZE), F32), pltpu.VMEM((2,) * 5 + (16, 256), BF), pltpu.VMEM((8, 128, 256), BF)]
        + [pltpu.VMEM((256, D), BF)]
        + rs_scratch(16, 1024, 3)
        + [pltpu.VMEM((4, 3, 16, 1024), BF)]
        + [pltpu.VMEM((2, 16, WIDE), BF), pltpu.VMEM((16, D), BF), pltpu.VMEM((16, WIDE), BF)]
        + [pltpu.VMEM(two + (32, w), BF) for w in WIDTHS]
        + [pltpu.VMEM((HALF, FFS), BF)] * 4
        + [pltpu.VMEM((FF, QUART), BF), pltpu.VMEM((1024, HALF), BF)]
        + [pltpu.VMEM((4, 256, 2 * FFS), BF)] * 2
        + [pltpu.VMEM((1024, FF), BF)]
        + rs_scratch(64, 256, 4)
        + [pltpu.VMEM((2, 4, 4, 16, 256), BF)]
        + [dma((2,)), dma((3, 2)), dma((4, 2))]
        + [dma((4, 3)), dma((4, 3)), dma((4, 3)), dma((4, 3)), dma((5,)), dma((5,)), dma((3,)), dma((1,)), dma((1,))]
        + [dma((6, 6, 6)), dma((6, 6, 6)), dma((4,)), dma((4,)), dma((3, 4)), dma((3, 4))]
        + [dma((4, 4)), dma((4, 4)), dma((4, 4)), dma((4, 4)), dma((7,)), dma((7,))]
    )
    return pl.pallas_call(
        kernel,
        out_shape=(
            jax.ShapeDtypeStruct((16, D), BF),
            jax.ShapeDtypeStruct((16, D), F32),
            jax.ShapeDtypeStruct((FFS, FF), F32),
        ),
        in_specs=[hbm] * 11,
        out_specs=(hbm, hbm, hbm),
        scratch_shapes=scratch,
        compiler_params=pltpu.CompilerParams(
            collective_id=0, has_side_effects=True, vmem_limit_bytes=62 * 2**20
        ),
        name="layer",
    )(q, ow, resid, gain, gate, rank, keys, values, wg, wu, wd)


def gray(a, axis):
    parts = [lax.slice_in_dim(a, i, i + 1, axis=axis) for i in GRAY]
    return jnp.concatenate(parts, axis=axis)


def gathered_order(a):
    rest = a.shape[1:]
    n = len(rest)
    a = a.reshape((2, 2, 4, 4, 2, 16) + rest)
    a = jnp.transpose(a, (2, 3, 0, 4, 1, 5) + tuple(range(6, 6 + n)))
    a = a.reshape((4, 4, 4, 32) + rest)
    for axis in range(3):
        a = gray(a, axis)
    return a.reshape((2048,) + rest)


def local(
    resid, query, keys, values, out_weight, post_gain, route_idx, gates, w_gate, w_up, w_down
):
    exp_pos = lax.axis_index("exp")
    block = lax.axis_index("ctx") * EXPERTS + exp_pos
    own_idx = lax.dynamic_slice_in_dim(route_idx, block * 16, 16, 0)
    expert = jnp.arange(128, dtype=jnp.int32)
    expert = jnp.where(expert < 3 * EXPERTS, expert % EXPERTS, -1)
    gate = jnp.sum(jnp.where(own_idx[:, :, None] == expert[None, None, :], gates[:, :, None], 0.0), axis=1)
    member = jnp.any(route_idx == exp_pos, axis=1)
    member = gathered_order(member.astype(BF)).reshape(128, 16)
    before = (jnp.arange(16)[:, None] < jnp.arange(16)[None, :]).astype(BF)
    rank = jnp.dot(member, before, preferred_element_type=F32)
    rank = jnp.where(member > 0, rank, -1.0).astype(jnp.int32).reshape(8, 1, 256)
    mixed, attn_out, gram = fused(
        query, out_weight, resid, post_gain.reshape(1, D), gate, rank, keys, values, w_gate[0], w_up[0], w_down[0]
    )
    return (mixed, attn_out, gram[None])


def solution(mesh):
    placed = (
        P(("ctx", "exp"), None),
        P("ctx", "exp"),
        P("ctx", None),
        P("ctx", None),
        P("exp", None),
        P(),
        P(),
        P(("ctx", "exp"), None),
        P("exp", None, "ctx"),
        P("exp", None, "ctx"),
        P("exp", "ctx", None),
    )
    return jax.shard_map(
        local,
        mesh=mesh,
        in_specs=placed,
        out_specs=(P(("ctx", "exp"), None), P(("ctx", "exp"), None), P("exp", "ctx", None)),
        check_vma=False,
    )
```

```python
import functools
import math

import jax
import jax.numpy as jnp
from jax import lax
from jax.experimental import pallas as pl
from jax.experimental.pallas import tpu as pltpu
from jax.sharding import PartitionSpec as P

EXPERTS = 32
HEAD_SIZE = 128
D = 4096
FF = 1536
FFS = 384
HALF = D // 2
QUART = D // 4
MESH = pl.DeviceIdType.MESH
BF = jnp.bfloat16
F32 = jnp.float32

RS_ORDER = ((0, 2, 1, 3, 4), (2, 1, 3, 0, 4), (1, 3, 0, 2, 4), (3, 0, 2, 1, 4))
CYCLE = (0, 2, 4, 1, 3, 5)
WIDTHS = (384, 384, 384, 384, 384, 256)
USED = (384, 384, 384, 384, 256, 256)
OFFS = (0, 384, 768, 1152, 1536, 1792)
WIDE = HALF + 128
GRAY = (0, 1, 3, 2)
ZMAP = ((0, 0), (1, 0), (1, 1), (0, 1))
FULL = slice(None)


def block_bits(i, n):
    return [(i // (2 ** (n - 1 - j))) % 2 for j in range(n)]


def kernel(
    q_hbm, ow_hbm, resid_hbm, gain_hbm, gate_hbm, rank_hbm, keys_ref, values_ref, wg_ref, wu_ref, wd_ref,
    mixed_ref, attn_ref, gram_hbm,
    q_ref, resid_ref, gain_ref, gate_ref, rank_ref, gram_ref, isem, osem,
    kk, vv, top_s, acc_s, h_ref, sel_ref, ow_ref,
    p1, r10, r11, r12, r13, norm, stream, csh, x0, x1, x2, x3, x4, x5,
    wgk, wuk, wgs, wus, wdq, xs, psend, precv, hall, p2, r20, r21, r22, r23, frecv,
    kvl, kvs, kvr,
    s1s, s1r, t1s, t1r, wss, wsr, lsem, ccs, ccr, ags, agr, pss, psr, hss, hsr, has, har, s2s, s2r, fss, fsr,
):
    c = lax.axis_index("ctx")
    e = lax.axis_index("exp")
    x, y, zl, zh, k = e // 8, (e // 2) % 4, e % 2, c // 2, c % 2

    def dev(x_, y_, zl_, zh_, k_):
        return (zh_ * 2 + k_, x_ * 8 + y_ * 2 + zl_)

    def flip1(v):
        return v + 1 - 2 * (v % 2)

    peer_x = (dev(3 - x, y, zl, zh, k), dev(flip1(x), y, zl, zh, k))
    peer_y = (dev(x, 3 - y, zl, zh, k), dev(x, flip1(y), zl, zh, k))
    peer_z1 = dev(x, y, 1 - zl, zh, k)
    peer_z3 = dev(x, y, 1 - zl, 1 - zh, k)
    sib = dev(x, y, zl, zh, 1 - k)
    far = dev(x, y, zl, 1 - zh, k)
    farsib = dev(x, y, zl, 1 - zh, 1 - k)
    rs_peer = (peer_x[0], peer_x[1], peer_y[0], peer_y[1], peer_z1)
    diagonal = (
        dev(3 - x, y, 1 - zl, zh, k), dev(flip1(x), y, 1 - zl, zh, k),
        dev(x, 3 - y, 1 - zl, zh, k), dev(x, flip1(y), 1 - zl, zh, k),
    )
    z1sib, z3sib = dev(x, y, 1 - zl, zh, 1 - k), dev(x, y, 1 - zl, 1 - zh, 1 - k)
    ag_peer = (peer_x[0], peer_x[1], peer_y[0], peer_y[1], peer_z3, peer_z1)
    xb1, yb1 = x // 2, y // 2
    own5 = (xb1, (xb1 + x % 2) % 2, yb1, (yb1 + y % 2) % 2, zl)
    own6 = own5[:4] + (zh, (zh + zl) % 2)

    hbm_vmem = (
        (q_hbm, q_ref), (rank_hbm, rank_ref), (ow_hbm, ow_ref), (resid_hbm, resid_ref), (gain_hbm, gain_ref),
        (gate_hbm, gate_ref),
    )
    input_copies = [pltpu.make_async_copy(a, b, isem.at[i]) for i, (a, b) in enumerate(hbm_vmem)]
    gram_copy = pltpu.make_async_copy(gram_ref, gram_hbm, osem.at[0])
    barrier = pltpu.get_barrier_semaphore()
    partners = list(ag_peer) + [sib, far, farsib, z1sib, z3sib] + list(diagonal)
    for p in partners:
        pl.semaphore_signal(barrier, inc=1, device_id=p, device_id_type=MESH)
    pl.semaphore_wait(barrier, len(partners))

    def remote(src, dst, ss, rs, to):
        return pltpu.make_async_remote_copy(
            src_ref=src, dst_ref=dst, send_sem=ss, recv_sem=rs, device_id=to, device_id_type=MESH
        )

    head_cols = pl.ds(pl.multiple_of(x * HEAD_SIZE, HEAD_SIZE), HEAD_SIZE)
    kv_src = (keys_ref.at[:, head_cols], values_ref.at[:, head_cols])

    def kv_dst(cc, j):
        return vv.at[cc, :, 0:HEAD_SIZE] if j else kk.at[cc]

    def kv_copy(i, to, cc, j):
        return remote(kv_src[j], kv_dst(cc, j), kvs.at[i, j], kvr.at[cc, j], to)

    def kv_local(j):
        return pltpu.make_async_copy(kv_src[j], kv_dst(c, j), kvl.at[j])

    def kv_forward(j):
        return remote(kv_dst(k, j), kv_dst(k, j), kvs.at[2, j], kvr.at[k, j], sib)

    for j in range(2):

        @pl.when(zh == 0)
        def _():
            kv_copy(1, peer_z3, c, j).start()

    for j in range(2):

        @pl.when(k == 0)
        def _():
            kv_copy(0, sib, c, j).start()

        kv_local(j).start()

    for cp in input_copies:
        cp.start()

    other = pl.ds(pl.multiple_of((1 - k) * HALF, HALF), HALF)
    mine = pl.ds(pl.multiple_of(k * HALF, HALF), HALF)
    own_rows = pl.ds(pl.multiple_of(c * FFS, FFS), FFS)

    def quarter(cc):
        return pl.ds(pl.multiple_of(cc * QUART, QUART), QUART)

    near_copies = [
        remote(wg_ref.at[other], wgs, wss.at[0], wsr.at[0], sib),
        remote(wu_ref.at[other], wus, wss.at[1], wsr.at[1], sib),
        remote(wd_ref.at[:, quarter(zh * 2 + 1 - k)], wdq.at[own_rows], wss.at[2], wsr.at[2], sib),
        pltpu.make_async_copy(wg_ref.at[mine], wgk, lsem.at[0]),
        pltpu.make_async_copy(wu_ref.at[mine], wuk, lsem.at[1]),
        pltpu.make_async_copy(wd_ref.at[:, quarter(c)], wdq.at[own_rows], lsem.at[2]),
    ]
    far_copies = [
        remote(wd_ref.at[:, quarter((1 - zh) * 2 + k)], wdq.at[own_rows], wss.at[3], wsr.at[3], far),
        remote(wd_ref.at[:, quarter((1 - zh) * 2 + 1 - k)], wdq.at[own_rows], wss.at[4], wsr.at[4], farsib),
    ]

    @pl.when(zh == 1)
    def _():
        for cp in far_copies:
            cp.start()

    slot = lax.broadcasted_iota(jnp.int32, (128, 256), 0)
    token = lax.broadcasted_iota(jnp.int32, (128, 256), 1)
    place = jnp.where(slot // 8 == token // 16, slot % 8, -2)

    for cp in input_copies[:2]:
        cp.wait()

    def pick_slots(g):
        sel_ref[g] = jnp.where(place == rank_ref[g], 1.0, 0.0).astype(BF)

    pl.loop(0, 8)(pick_slots)
    for cc in range(4):
        vv[cc, :, HEAD_SIZE:] = jnp.ones((512, HEAD_SIZE), BF)
    scale = math.log2(math.e) / math.sqrt(HEAD_SIZE)
    trans = (((1,), (1,)), ((), ()))

    def queries(t):
        rows = slice(t * 128, t * 128 + 128)
        return jnp.concatenate([q_ref[rows, :HEAD_SIZE], q_ref[rows, HEAD_SIZE:]], axis=0)

    for j in range(2):
        kv_local(j).wait()
    for t in range(4):
        n = t * 128 + 128
        scores = lax.dot_general(queries(t), kk[c, :n], trans, preferred_element_type=F32)
        q_place = lax.rem(lax.broadcasted_iota(jnp.int32, (256, n), 0), 128) + t * 128
        scores = jnp.where(q_place >= lax.broadcasted_iota(jnp.int32, (256, n), 1), scores, -1e30)
        new = jnp.max(scores, axis=1, keepdims=True)
        w = jnp.exp2((scores - new) * scale).astype(BF)
        top_s[t] = new
        acc_s[t] = jnp.dot(w, vv[c, :n], preferred_element_type=F32)

    @pl.when(zh == 1)
    def _():
        for j in range(2):
            kv_copy(1, peer_z3, k, j).wait_recv()
            kv_forward(j).start()

    for cp in near_copies:
        cp.start()

    def key_block(i):
        cc = c - i

        @pl.when(jnp.logical_or(zh == 0, cc != k))
        def _():
            for j in range(2):
                kv_copy(0, sib, cc, j).wait_recv()

        for t in range(4):
            scores = lax.dot_general(queries(t), kk[cc], trans, preferred_element_type=F32)
            old = top_s[t]
            new = jnp.maximum(old, jnp.max(scores, axis=1, keepdims=True))
            w = jnp.exp2((scores - new) * scale).astype(BF)
            fade = jnp.exp2((old - new) * scale)
            top_s[t] = new
            acc_s[t] = acc_s[t] * fade + jnp.dot(w, vv[cc], preferred_element_type=F32)

    pl.loop(1, c + 1)(key_block)

    @pl.when(zh == 0)
    def _():
        for cp in far_copies:
            cp.start()

    def head_tile(t):
        out = (acc_s[t, :, :HEAD_SIZE] / acc_s[t, :, HEAD_SIZE:]).astype(BF)
        b1 = t // 2
        b0 = (b1 + t % 2) % 2
        for hd in range(2):
            for yy in range(4):
                at = hd * 128 + yy * 32
                h_ref[b1, b0, yy // 2, (yy // 2 + yy) % 2, :, :, hd * 128 : hd * 128 + 128] = out[at : at + 32].reshape(2, 16, 128)

    pl.loop(0, 4)(head_tile)

    def rs_index(f, s, bit):
        order = RS_ORDER[f]
        idx = [FULL] * 5
        for d in order[:s]:
            idx[d] = own5[d]
        idx[order[s]] = bit
        return tuple(idx)

    def rs_copy(buf, recv, ss, rs, f, s):
        d = RS_ORDER[f][s]
        return remote(
            buf.at[(f,) + rs_index(f, s, 1 - own5[d])], recv[s].at[f], ss.at[f, s], rs.at[f, s], rs_peer[d]
        )

    def rs_add(buf, recv, f, s, bit):
        order = RS_ORDER[f]
        step = order[s + 1]
        left = sorted(order[s + 2 :])
        n = len(left)

        def one(i):
            bits = dict(zip(left, block_bits(i, n)))
            bits[step] = bit
            idx = list(own5)
            for d in bits:
                idx[d] = bits[d]
            idx = (f,) + tuple(idx)
            got = recv[s][(f,) + tuple(bits[d] for d in sorted(bits))]
            buf[idx] = (buf[idx].astype(F32) + got.astype(F32)).astype(BF)

        if n:
            pl.loop(0, 2**n)(one)
        else:
            one(0)

    recv1 = (r10, r11, r12)
    recv2 = (r20, r21, r22, r23)

    def project(f, bit):
        idx = rs_index(f, 0, bit)
        rows = h_ref[idx].reshape(256, 256)
        for t in range(2):
            cols = f * 1024 + t * 512
            out = jnp.dot(rows, ow_ref[:, cols : cols + 512], preferred_element_type=F32)
            p1[(f,) + idx + (FULL, slice(t * 512, t * 512 + 512))] = out.astype(BF).reshape(2, 2, 2, 2, 16, 512)

    for cp in input_copies[2:]:
        cp.wait()
    first = []
    for f in range(4):
        project(f, 1 - own5[RS_ORDER[f][0]])
        cp = rs_copy(p1, recv1, s1s, s1r, f, 0)
        cp.start()
        first.append(cp)

    for f in range(4):
        project(f, own5[RS_ORDER[f][0]])
    for j in range(2):

        @pl.when(zh == 0)
        def _():
            kv_copy(1, peer_z3, c, j).wait_send()

        @pl.when(zh == 1)
        def _():
            kv_forward(j).wait_send()

        @pl.when(k == 0)
        def _():
            kv_copy(0, sib, c, j).wait_send()

    def run_rs(buf, recv, ss, rs, wait_first, steps, tail):
        last = [None] * 4
        for s in range(steps):
            for f in range(4):
                if s == 0:
                    wait_first(f)
                else:
                    last[f].wait()
                d = RS_ORDER[f][s + 1]
                rs_add(buf, recv, f, s, 1 - own5[d])
                if s + 1 < steps:
                    last[f] = rs_copy(buf, recv, ss, rs, f, s + 1)
                    last[f].start()
                rs_add(buf, recv, f, s, own5[d])
                if s + 1 == steps:
                    tail(f)

    tails = []

    def direct(f):
        d = RS_ORDER[f][3]
        for i, (to, flips) in enumerate(((rs_peer[d], (d,)), (peer_z1, (4,)), (diagonal[d], (d, 4)))):
            idx = tuple(1 - own5[j] if j in flips else own5[j] for j in range(5))
            cp = remote(p1.at[(f,) + idx], r13.at[f, i], t1s.at[f, i], t1r.at[f, i], to)
            cp.start()
            tails.append(cp)

    run_rs(p1, recv1, s1s, s1r, lambda f: first[f].wait(), 3, direct)
    parts = []
    for f in range(4):
        for i in range(3):
            tails[f * 3 + i].wait()
        got = [r13[f, i].astype(F32) for i in range(3)]
        parts.append((p1[(f,) + own5].astype(F32) + got[0]) + (got[1] + got[2]))

    squares = jnp.zeros((16, 1), F32)
    for f in range(4):
        cols = slice(f * 1024, f * 1024 + 1024)
        attn_ref[:, cols] = parts[f]
        st = (resid_ref[:, cols].astype(F32) + parts[f]).astype(BF)
        stream[:, cols] = st
        sf = st.astype(F32)
        squares = squares + jnp.sum(sf * sf, axis=1, keepdims=True)
    inv = lax.rsqrt(squares / D + 1e-06)
    for f in range(4):
        cols = slice(f * 1024, f * 1024 + 1024)
        out = (stream[:, cols].astype(F32) * inv * gain_ref[:, cols]).astype(BF)
        norm[f // 2, :, (f % 2) * 1024 : (f % 2) * 1024 + 1024] = out
    gates = gate_ref[...]
    top = gates.astype(BF)
    rest = gates - top.astype(F32)
    middle = rest.astype(BF)
    low = (rest - middle.astype(F32)).astype(BF)
    lane = lax.broadcasted_iota(jnp.int32, (16, 128), 1)
    gates = jnp.where(lane < EXPERTS, top.astype(F32), jnp.where(lane < 2 * EXPERTS, middle.astype(F32), low.astype(F32)))
    for i in range(2):
        norm[i, :, HALF:] = gates.astype(BF)

    xf = (x0, x1, x2, x3, x4, x5)
    swap = remote(norm.at[1 - k], csh, ccs.at[0], ccr.at[0], sib)
    swap.start()
    own_tok = pl.ds(pl.multiple_of(k * 16, 16), 16)
    sib_tok = pl.ds(pl.multiple_of((1 - k) * 16, 16), 16)
    for f in range(6):
        xf[f][own6 + (own_tok, slice(0, USED[f]))] = norm[k, :, OFFS[f] : OFFS[f] + USED[f]]
    x4[own6 + (own_tok, slice(256, 384))] = norm[k, :, HALF:]
    swap.wait()
    for f in range(6):
        xf[f][own6 + (sib_tok, slice(0, USED[f]))] = csh[:, OFFS[f] : OFFS[f] + USED[f]]
    x4[own6 + (sib_tok, slice(256, 384))] = csh[:, HALF:]

    def ag_copy(f, s, j):
        idx = list(own6)
        for t in range(j):
            idx[CYCLE[(f + t) % 6]] = FULL
        if j >= 0:
            d = CYCLE[(f + j) % 6]
            idx[d] = 1 - own6[d]
        part = xf[f].at[tuple(idx)]
        return remote(part, part, ags.at[f, s, j + 1], agr.at[f, s, j + 1], ag_peer[CYCLE[(f + s) % 6]])

    for s in range(6):
        for f in range(6):
            ag_copy(f, s, -1).start()
    for s in range(6):
        for f in range(6):
            for j in range(-1, s):
                ag_copy(f, s, j).wait_recv()
            for t in range(s + 1, 6):
                ag_copy(f, t, s).start()
    for s in range(6):
        for f in range(6):
            for j in range(-1, s):
                ag_copy(f, s, j).wait_send()

    for cp in near_copies + far_copies:
        cp.wait()

    def chunk_bits(i):
        return (1 - own5[0] + i // 2) % 2, (1 - own5[1] + i % 2) % 2

    def chunk(i):
        b1, b0 = chunk_bits(i)
        return b1 * 2 + b0

    def chunk_rows(m):
        return pl.ds(pl.multiple_of(m * 256, 256), 256)

    def select(m):
        for g in range(2):
            pick = sel_ref[m * 2 + g]
            rows = pl.ds(pl.multiple_of(m * 256 + g * 128, 128), 128)
            for f in range(6):
                block = xf[f][m // 2, m % 2, g].reshape(256, WIDTHS[f])[:, : USED[f]]
                xs[rows, OFFS[f] : OFFS[f] + USED[f]] = jnp.dot(pick, block, preferred_element_type=F32).astype(BF)

    def partial_copy(m):
        return remote(psend.at[m], precv.at[m], pss.at[m], psr.at[m], sib)

    def other_units(m):
        a = xs[chunk_rows(m), :]
        psend[m, :, :FFS] = jnp.dot(a, wgs[...], preferred_element_type=F32).astype(BF)
        psend[m, :, FFS:] = jnp.dot(a, wus[...], preferred_element_type=F32).astype(BF)
        partial_copy(m).start()

    def hidden_cols(cc):
        return pl.ds(pl.multiple_of(cc * FFS, 128), FFS)

    def hidden_copy(m, cc, kind, to):
        part = hall.at[chunk_rows(m), hidden_cols(cc)]
        return remote(part, part, hss.at[kind, m], hsr.at[kind, m], to)

    def own_units(m):
        a = xs[chunk_rows(m), :]
        gate = jnp.dot(a, wgk[...], preferred_element_type=F32)
        upper = jnp.dot(a, wuk[...], preferred_element_type=F32)
        partial_copy(m).wait()
        gate = gate + precv[m, :, :FFS].astype(F32)
        upper = upper + precv[m, :, FFS:].astype(F32)
        hall[chunk_rows(m), hidden_cols(c)] = (gate / (1.0 + jnp.exp(-gate)) * upper).astype(BF)
        hidden_copy(m, c, 0, far).start()
        hidden_copy(m, c, 1, sib).start()

    def units(i):
        @pl.when(i < 4)
        def _():
            m = chunk(i)
            select(m)
            other_units(m)

        @pl.when(i > 0)
        def _():
            own_units(chunk(i - 1))

    pl.loop(0, 5)(units)
    far_c = (1 - zh) * 2 + k

    def half_copy(f, b1, b0):
        if f == 0:
            src, dst, sem = p2.at[0, b1, b0], r20.at[0, b0], b0
        elif f == 2:
            src, dst, sem = p2.at[2, b1, b0], r20.at[2, b1], b1
        elif f == 1:
            src, dst, sem = p2.at[1, b1, b0, 1 - own5[2]], r20.at[1, b1, b0], b1 * 2 + b0
        else:
            src, dst, sem = p2.at[3, b1, b0, :, 1 - own5[3]], r20.at[3, b1, b0], b1 * 2 + b0
        return remote(src, dst, has.at[f, sem], har.at[f, sem], rs_peer[RS_ORDER[f][0]])

    lane = lax.broadcasted_iota(jnp.int32, (256, 128), 1)
    my_lanes = jnp.logical_or(lane == e, jnp.logical_or(lane == e + EXPERTS, lane == e + 2 * EXPERTS))

    def down(i):
        b1, b0 = chunk_bits(i)
        m = b1 * 2 + b0
        hidden_copy(m, c, 1, sib).wait()
        hidden_copy(m, far_c, 2, sib).wait()
        a = hall[chunk_rows(m), :]
        weights = []
        for g in range(2):
            block = x4[b1, b0, g].reshape(256, 384)[:, 256:].astype(F32)
            weights.append(jnp.sum(jnp.where(my_lanes, block, 0.0), axis=1, keepdims=True))
        for f in range(4):
            cols = slice(f * 256, f * 256 + 256)
            out = jnp.dot(a, wdq[:, cols], preferred_element_type=F32).astype(BF)
            for g in range(2):
                tok = lax.dot_general(
                    sel_ref[m * 2 + g], out[g * 128 : g * 128 + 128], (((0,), (0,)), ((), ())),
                    preferred_element_type=F32,
                )
                tok = (tok * weights[g]).astype(BF)
                for yb in range(2):
                    for j in range(4):
                        zlo, zhi = ZMAP[j]
                        at = (yb * 4 + j) * 32
                        p2[f, b1, b0, g, yb, zlo, zhi * 32 : zhi * 32 + 32, :] = tok[at : at + 32]
            if f == 0:
                pl.when(i < 2)(lambda: half_copy(0, b1, b0).start())
            elif f == 2:
                pl.when(i % 2 == 0)(lambda: half_copy(2, b1, b0).start())
            else:
                half_copy(f, b1, b0).start()

    def spread(i):
        @pl.when(i < 4)
        def _():
            m = chunk(i)
            hidden_copy(m, c, 0, far).wait()
            hidden_copy(m, far_c, 2, sib).start()

        @pl.when(i > 0)
        def _():
            down(i - 1)

    pl.loop(0, 5)(spread)

    def wait_half(f):
        for b in range(2 if f % 2 == 0 else 4):
            if f == 0:
                half_copy(0, 1 - own5[0], b).wait()
            elif f == 2:
                half_copy(2, b, 1 - own5[1]).wait()
            else:
                half_copy(f, b // 2, b % 2).wait()

    count = jnp.sum(jnp.where(rank_ref[:, 0, :] >= 0, 1.0, 0.0))

    def gram(j):
        cols = pl.ds(pl.multiple_of(j * 256, 256), 256)
        out = lax.dot_general(
            hall[:, hidden_cols(c)], hall[:, cols], (((0,), (0,)), ((), ())), preferred_element_type=F32
        )
        gram_ref[:, cols] = out / count

    pl.loop(0, 6)(gram)
    gram_copy.start()

    def nothing(f):
        return None

    run_rs(p2, recv2, s2s, s2r, wait_half, 4, nothing)
    final = []
    for i, (to, (flip_l, flip_h, flip_k)) in enumerate(
        (
            (sib, (0, 0, 1)), (peer_z1, (1, 0, 0)), (far, (0, 1, 0)), (peer_z3, (1, 1, 0)),
            (z1sib, (1, 0, 1)), (farsib, (0, 1, 1)), (z3sib, (1, 1, 1)),
        )
    ):
        to_l = 1 - zl if flip_l else zl
        to_c = (1 - zh if flip_h else zh) * 2 + (1 - k if flip_k else k)
        rows = pl.ds(pl.multiple_of(to_c * 16, 16), 16)
        cp = remote(p2.at[(FULL,) + own5[:4] + (to_l, rows)], frecv.at[zl, c], fss.at[i], fsr.at[i], to)
        cp.start()
        final.append(cp)
    rows = pl.ds(pl.multiple_of(c * 16, 16), 16)
    frecv[zl, c] = p2[(FULL,) + own5 + (rows,)]
    for cp in final:
        cp.wait()
    for cc in range(4):
        for f in range(4):
            cols = slice(cc * QUART + f * 256, cc * QUART + f * 256 + 256)
            routed = frecv[0, cc, f].astype(F32) + frecv[1, cc, f].astype(F32)
            mixed_ref[:, cols] = (stream[:, cols].astype(F32) + routed).astype(BF)
    gram_copy.wait()


def fused(q, ow, resid, gain, gate, rank, keys, values, wg, wu, wd):
    dma = pltpu.SemaphoreType.DMA
    vm = pl.BlockSpec(memory_space=pltpu.VMEM)
    hbm = pl.BlockSpec(memory_space=pl.ANY)
    two = (2,) * 6

    def rs_scratch(rows, cols, steps):
        out = [pltpu.VMEM((4,) + (2,) * 5 + (rows, cols), BF)]
        for s in range(steps):
            out.append(pltpu.VMEM((4,) + (2,) * (4 - s) + (rows, cols), BF))
        return out

    scratch = (
        [pltpu.VMEM((512, 256), BF), pltpu.VMEM((16, D), BF), pltpu.VMEM((1, D), F32), pltpu.VMEM((16, 128), F32)]
        + [pltpu.VMEM((8, 1, 256), jnp.int32), pltpu.VMEM((FFS, FF), F32), dma((6,)), dma((1,))]
        + [pltpu.VMEM((4, 512, HEAD_SIZE), BF), pltpu.VMEM((4, 512, 2 * HEAD_SIZE), BF), pltpu.VMEM((4, 256, 1), F32)]
        + [pltpu.VMEM((4, 256, 2 * HEAD_SIZE), F32), pltpu.VMEM((2,) * 5 + (16, 256), BF), pltpu.VMEM((8, 128, 256), BF)]
        + [pltpu.VMEM((256, D), BF)]
        + rs_scratch(16, 1024, 3)
        + [pltpu.VMEM((4, 3, 16, 1024), BF)]
        + [pltpu.VMEM((2, 16, WIDE), BF), pltpu.VMEM((16, D), BF), pltpu.VMEM((16, WIDE), BF)]
        + [pltpu.VMEM(two + (32, w), BF) for w in WIDTHS]
        + [pltpu.VMEM((HALF, FFS), BF)] * 4
        + [pltpu.VMEM((FF, QUART), BF), pltpu.VMEM((1024, HALF), BF)]
        + [pltpu.VMEM((4, 256, 2 * FFS), BF)] * 2
        + [pltpu.VMEM((1024, FF), BF)]
        + rs_scratch(64, 256, 4)
        + [pltpu.VMEM((2, 4, 4, 16, 256), BF)]
        + [dma((2,)), dma((3, 2)), dma((4, 2))]
        + [dma((4, 3)), dma((4, 3)), dma((4, 3)), dma((4, 3)), dma((5,)), dma((5,)), dma((3,)), dma((1,)), dma((1,))]
        + [dma((6, 6, 6)), dma((6, 6, 6)), dma((4,)), dma((4,)), dma((3, 4)), dma((3, 4))]
        + [dma((4, 4)), dma((4, 4)), dma((4, 4)), dma((4, 4)), dma((7,)), dma((7,))]
    )
    return pl.pallas_call(
        kernel,
        out_shape=(
            jax.ShapeDtypeStruct((16, D), BF),
            jax.ShapeDtypeStruct((16, D), F32),
            jax.ShapeDtypeStruct((FFS, FF), F32),
        ),
        in_specs=[hbm] * 11,
        out_specs=(vm, vm, hbm),
        scratch_shapes=scratch,
        compiler_params=pltpu.CompilerParams(
            collective_id=0, has_side_effects=True, vmem_limit_bytes=62 * 2**20
        ),
        name="layer",
    )(q, ow, resid, gain, gate, rank, keys, values, wg, wu, wd)


def gray(a, axis):
    parts = [lax.slice_in_dim(a, i, i + 1, axis=axis) for i in GRAY]
    return jnp.concatenate(parts, axis=axis)


def gathered_order(a):
    rest = a.shape[1:]
    n = len(rest)
    a = a.reshape((2, 2, 4, 4, 2, 16) + rest)
    a = jnp.transpose(a, (2, 3, 0, 4, 1, 5) + tuple(range(6, 6 + n)))
    a = a.reshape((4, 4, 4, 32) + rest)
    for axis in range(3):
        a = gray(a, axis)
    return a.reshape((2048,) + rest)


def local(
    resid, query, keys, values, out_weight, post_gain, route_idx, gates, w_gate, w_up, w_down
):
    exp_pos = lax.axis_index("exp")
    block = lax.axis_index("ctx") * EXPERTS + exp_pos
    own_idx = lax.dynamic_slice_in_dim(route_idx, block * 16, 16, 0)
    expert = jnp.arange(128, dtype=jnp.int32)
    expert = jnp.where(expert < 3 * EXPERTS, expert % EXPERTS, -1)
    gate = jnp.sum(jnp.where(own_idx[:, :, None] == expert[None, None, :], gates[:, :, None], 0.0), axis=1)
    member = jnp.any(route_idx == exp_pos, axis=1)
    member = gathered_order(member.astype(BF)).reshape(128, 16)
    before = (jnp.arange(16)[:, None] < jnp.arange(16)[None, :]).astype(BF)
    rank = jnp.dot(member, before, preferred_element_type=F32)
    rank = jnp.where(member > 0, rank, -1.0).astype(jnp.int32).reshape(8, 1, 256)
    mixed, attn_out, gram = fused(
        query, out_weight, resid, post_gain.reshape(1, D), gate, rank, keys, values, w_gate[0], w_up[0], w_down[0]
    )
    return (mixed, attn_out, gram[None])


def solution(mesh):
    placed = (
        P(("ctx", "exp"), None),
        P("ctx", "exp"),
        P("ctx", None),
        P("ctx", None),
        P("exp", None),
        P(),
        P(),
        P(("ctx", "exp"), None),
        P("exp", None, "ctx"),
        P("exp", None, "ctx"),
        P("exp", "ctx", None),
    )
    return jax.shard_map(
        local,
        mesh=mesh,
        in_specs=placed,
        out_specs=(P(("ctx", "exp"), None), P(("ctx", "exp"), None), P("exp", "ctx", None)),
        check_vma=False,
    )
```

```python
import functools
import math

import jax
import jax.numpy as jnp
from jax import lax
from jax.experimental import pallas as pl
from jax.experimental.pallas import tpu as pltpu
from jax.sharding import PartitionSpec as P

EXPERTS = 32
HEAD_SIZE = 128
D = 4096
FF = 1536
FFS = 384
HALF = D // 2
QUART = D // 4
MESH = pl.DeviceIdType.MESH
BF = jnp.bfloat16
F32 = jnp.float32

RS_ORDER = ((0, 2, 1, 3, 4), (2, 1, 3, 0, 4), (1, 3, 0, 2, 4), (3, 0, 2, 1, 4))
CYCLE = (0, 2, 4, 1, 3, 5)
WIDTHS = (384, 384, 384, 384, 384, 256)
USED = (384, 384, 384, 384, 256, 256)
OFFS = (0, 384, 768, 1152, 1536, 1792)
WIDE = HALF + 128
GRAY = (0, 1, 3, 2)
ZMAP = ((0, 0), (1, 0), (1, 1), (0, 1))
FULL = slice(None)


def block_bits(i, n):
    return [(i // (2 ** (n - 1 - j))) % 2 for j in range(n)]


def kernel(
    q_hbm, ow_hbm, resid_hbm, gain_hbm, gate_hbm, rank_hbm, keys_ref, values_ref, wg_ref, wu_ref, wd_ref,
    mixed_ref, attn_ref, gram_ref,
    q_ref, resid_ref, gain_ref, gate_ref, rank_ref, isem,
    kk, vv, top_s, acc_s, h_ref, sel_ref, ow_ref,
    p1, r10, r11, r12, r13, norm, stream, csh, x0, x1, x2, x3, x4, x5,
    wgk, wuk, wgs, wus, wdq, xs, psend, precv, hall, p2, r20, r21, r22, r23, frecv,
    kvl, kvs, kvr,
    s1s, s1r, t1s, t1r, wss, wsr, lsem, ccs, ccr, ags, agr, pss, psr, hss, hsr, has, har, s2s, s2r, fss, fsr,
):
    c = lax.axis_index("ctx")
    e = lax.axis_index("exp")
    x, y, zl, zh, k = e // 8, (e // 2) % 4, e % 2, c // 2, c % 2

    def dev(x_, y_, zl_, zh_, k_):
        return (zh_ * 2 + k_, x_ * 8 + y_ * 2 + zl_)

    def flip1(v):
        return v + 1 - 2 * (v % 2)

    peer_x = (dev(3 - x, y, zl, zh, k), dev(flip1(x), y, zl, zh, k))
    peer_y = (dev(x, 3 - y, zl, zh, k), dev(x, flip1(y), zl, zh, k))
    peer_z1 = dev(x, y, 1 - zl, zh, k)
    peer_z3 = dev(x, y, 1 - zl, 1 - zh, k)
    sib = dev(x, y, zl, zh, 1 - k)
    far = dev(x, y, zl, 1 - zh, k)
    farsib = dev(x, y, zl, 1 - zh, 1 - k)
    rs_peer = (peer_x[0], peer_x[1], peer_y[0], peer_y[1], peer_z1)
    diagonal = (
        dev(3 - x, y, 1 - zl, zh, k), dev(flip1(x), y, 1 - zl, zh, k),
        dev(x, 3 - y, 1 - zl, zh, k), dev(x, flip1(y), 1 - zl, zh, k),
    )
    z1sib, z3sib = dev(x, y, 1 - zl, zh, 1 - k), dev(x, y, 1 - zl, 1 - zh, 1 - k)
    ag_peer = (peer_x[0], peer_x[1], peer_y[0], peer_y[1], peer_z3, peer_z1)
    xb1, yb1 = x // 2, y // 2
    own5 = (xb1, (xb1 + x % 2) % 2, yb1, (yb1 + y % 2) % 2, zl)
    own6 = own5[:4] + (zh, (zh + zl) % 2)

    hbm_vmem = (
        (q_hbm, q_ref), (rank_hbm, rank_ref), (ow_hbm, ow_ref), (resid_hbm, resid_ref), (gain_hbm, gain_ref),
        (gate_hbm, gate_ref),
    )
    input_copies = [pltpu.make_async_copy(a, b, isem.at[i]) for i, (a, b) in enumerate(hbm_vmem)]
    barrier = pltpu.get_barrier_semaphore()
    partners = list(ag_peer) + [sib, far, farsib, z1sib, z3sib] + list(diagonal)
    for p in partners:
        pl.semaphore_signal(barrier, inc=1, device_id=p, device_id_type=MESH)
    pl.semaphore_wait(barrier, len(partners))

    def remote(src, dst, ss, rs, to):
        return pltpu.make_async_remote_copy(
            src_ref=src, dst_ref=dst, send_sem=ss, recv_sem=rs, device_id=to, device_id_type=MESH
        )

    head_cols = pl.ds(pl.multiple_of(x * HEAD_SIZE, HEAD_SIZE), HEAD_SIZE)
    kv_src = (keys_ref.at[:, head_cols], values_ref.at[:, head_cols])

    def kv_dst(cc, j):
        return vv.at[cc, :, 0:HEAD_SIZE] if j else kk.at[cc]

    def kv_copy(i, to, cc, j):
        return remote(kv_src[j], kv_dst(cc, j), kvs.at[i, j], kvr.at[cc, j], to)

    def kv_local(j):
        return pltpu.make_async_copy(kv_src[j], kv_dst(c, j), kvl.at[j])

    def kv_forward(j):
        return remote(kv_dst(k, j), kv_dst(k, j), kvs.at[2, j], kvr.at[k, j], sib)

    for j in range(2):

        @pl.when(zh == 0)
        def _():
            kv_copy(1, far, c, j).start()
            kv_copy(2, farsib, c, j).start()

    for j in range(2):

        @pl.when(k == 0)
        def _():
            kv_copy(0, sib, c, j).start()

        kv_local(j).start()

    for cp in input_copies:
        cp.start()

    other = pl.ds(pl.multiple_of((1 - k) * HALF, HALF), HALF)
    mine = pl.ds(pl.multiple_of(k * HALF, HALF), HALF)
    own_rows = pl.ds(pl.multiple_of(c * FFS, FFS), FFS)

    def quarter(cc):
        return pl.ds(pl.multiple_of(cc * QUART, QUART), QUART)

    near_copies = [
        remote(wg_ref.at[other], wgs, wss.at[0], wsr.at[0], sib),
        remote(wu_ref.at[other], wus, wss.at[1], wsr.at[1], sib),
        remote(wd_ref.at[:, quarter(zh * 2 + 1 - k)], wdq.at[own_rows], wss.at[2], wsr.at[2], sib),
        pltpu.make_async_copy(wg_ref.at[mine], wgk, lsem.at[0]),
        pltpu.make_async_copy(wu_ref.at[mine], wuk, lsem.at[1]),
        pltpu.make_async_copy(wd_ref.at[:, quarter(c)], wdq.at[own_rows], lsem.at[2]),
    ]
    far_copies = [
        remote(wd_ref.at[:, quarter((1 - zh) * 2 + k)], wdq.at[own_rows], wss.at[3], wsr.at[3], far),
        remote(wd_ref.at[:, quarter((1 - zh) * 2 + 1 - k)], wdq.at[own_rows], wss.at[4], wsr.at[4], farsib),
    ]

    @pl.when(zh == 1)
    def _():
        for cp in far_copies:
            cp.start()

    slot = lax.broadcasted_iota(jnp.int32, (128, 256), 0)
    token = lax.broadcasted_iota(jnp.int32, (128, 256), 1)
    place = jnp.where(slot // 8 == token // 16, slot % 8, -2)

    for cp in input_copies[:2]:
        cp.wait()

    def pick_slots(g):
        sel_ref[g] = jnp.where(place == rank_ref[g], 1.0, 0.0).astype(BF)

    pl.loop(0, 8)(pick_slots)
    for cc in range(4):
        vv[cc, :, HEAD_SIZE:] = jnp.ones((512, HEAD_SIZE), BF)
    scale = math.log2(math.e) / math.sqrt(HEAD_SIZE)
    trans = (((1,), (1,)), ((), ()))

    def queries(t):
        rows = slice(t * 128, t * 128 + 128)
        return jnp.concatenate([q_ref[rows, :HEAD_SIZE], q_ref[rows, HEAD_SIZE:]], axis=0)

    for j in range(2):
        kv_local(j).wait()
    for t in range(4):
        n = t * 128 + 128
        scores = lax.dot_general(queries(t), kk[c, :n], trans, preferred_element_type=F32)
        q_place = lax.rem(lax.broadcasted_iota(jnp.int32, (256, n), 0), 128) + t * 128
        scores = jnp.where(q_place >= lax.broadcasted_iota(jnp.int32, (256, n), 1), scores, -1e30)
        new = jnp.max(scores, axis=1, keepdims=True)
        w = jnp.exp2((scores - new) * scale).astype(BF)
        top_s[t] = new
        acc_s[t] = jnp.dot(w, vv[c, :n], preferred_element_type=F32)

    for cp in near_copies:
        cp.start()

    def key_block(i):
        cc = c - i

        for j in range(2):
            kv_copy(0, sib, cc, j).wait_recv()

        for t in range(4):
            scores = lax.dot_general(queries(t), kk[cc], trans, preferred_element_type=F32)
            old = top_s[t]
            new = jnp.maximum(old, jnp.max(scores, axis=1, keepdims=True))
            w = jnp.exp2((scores - new) * scale).astype(BF)
            fade = jnp.exp2((old - new) * scale)
            top_s[t] = new
            acc_s[t] = acc_s[t] * fade + jnp.dot(w, vv[cc], preferred_element_type=F32)

    pl.loop(1, c + 1)(key_block)

    @pl.when(zh == 0)
    def _():
        for cp in far_copies:
            cp.start()

    def head_tile(t):
        out = (acc_s[t, :, :HEAD_SIZE] / acc_s[t, :, HEAD_SIZE:]).astype(BF)
        b1 = t // 2
        b0 = (b1 + t % 2) % 2
        for hd in range(2):
            for yy in range(4):
                at = hd * 128 + yy * 32
                h_ref[b1, b0, yy // 2, (yy // 2 + yy) % 2, :, :, hd * 128 : hd * 128 + 128] = out[at : at + 32].reshape(2, 16, 128)

    pl.loop(0, 4)(head_tile)

    def rs_index(f, s, bit):
        order = RS_ORDER[f]
        idx = [FULL] * 5
        for d in order[:s]:
            idx[d] = own5[d]
        idx[order[s]] = bit
        return tuple(idx)

    def rs_copy(buf, recv, ss, rs, f, s):
        d = RS_ORDER[f][s]
        return remote(
            buf.at[(f,) + rs_index(f, s, 1 - own5[d])], recv[s].at[f], ss.at[f, s], rs.at[f, s], rs_peer[d]
        )

    def rs_add(buf, recv, f, s, bit):
        order = RS_ORDER[f]
        step = order[s + 1]
        left = sorted(order[s + 2 :])
        n = len(left)

        def one(i):
            bits = dict(zip(left, block_bits(i, n)))
            bits[step] = bit
            idx = list(own5)
            for d in bits:
                idx[d] = bits[d]
            idx = (f,) + tuple(idx)
            got = recv[s][(f,) + tuple(bits[d] for d in sorted(bits))]
            buf[idx] = (buf[idx].astype(F32) + got.astype(F32)).astype(BF)

        if n:
            pl.loop(0, 2**n)(one)
        else:
            one(0)

    recv1 = (r10, r11, r12)
    recv2 = (r20, r21, r22, r23)

    def project(f, bit):
        idx = rs_index(f, 0, bit)
        rows = h_ref[idx].reshape(256, 256)
        for t in range(2):
            cols = f * 1024 + t * 512
            out = jnp.dot(rows, ow_ref[:, cols : cols + 512], preferred_element_type=F32)
            p1[(f,) + idx + (FULL, slice(t * 512, t * 512 + 512))] = out.astype(BF).reshape(2, 2, 2, 2, 16, 512)

    for cp in input_copies[2:]:
        cp.wait()
    first = []
    for f in range(4):
        project(f, 1 - own5[RS_ORDER[f][0]])
        cp = rs_copy(p1, recv1, s1s, s1r, f, 0)
        cp.start()
        first.append(cp)

    for f in range(4):
        project(f, own5[RS_ORDER[f][0]])
    for j in range(2):

        @pl.when(zh == 0)
        def _():
            kv_copy(1, far, c, j).wait_send()
            kv_copy(2, farsib, c, j).wait_send()

        @pl.when(k == 0)
        def _():
            kv_copy(0, sib, c, j).wait_send()

    def run_rs(buf, recv, ss, rs, wait_first, steps, tail):
        last = [None] * 4
        for s in range(steps):
            for f in range(4):
                if s == 0:
                    wait_first(f)
                else:
                    last[f].wait()
                d = RS_ORDER[f][s + 1]
                rs_add(buf, recv, f, s, 1 - own5[d])
                if s + 1 < steps:
                    last[f] = rs_copy(buf, recv, ss, rs, f, s + 1)
                    last[f].start()
                rs_add(buf, recv, f, s, own5[d])
                if s + 1 == steps:
                    tail(f)

    tails = []

    def direct(f):
        d = RS_ORDER[f][3]
        for i, (to, flips) in enumerate(((rs_peer[d], (d,)), (peer_z1, (4,)), (diagonal[d], (d, 4)))):
            idx = tuple(1 - own5[j] if j in flips else own5[j] for j in range(5))
            cp = remote(p1.at[(f,) + idx], r13.at[f, i], t1s.at[f, i], t1r.at[f, i], to)
            cp.start()
            tails.append(cp)

    run_rs(p1, recv1, s1s, s1r, lambda f: first[f].wait(), 3, direct)
    parts = []
    for f in range(4):
        for i in range(3):
            tails[f * 3 + i].wait()
        got = [r13[f, i].astype(F32) for i in range(3)]
        parts.append((p1[(f,) + own5].astype(F32) + got[0]) + (got[1] + got[2]))

    squares = jnp.zeros((16, 1), F32)
    for f in range(4):
        cols = slice(f * 1024, f * 1024 + 1024)
        attn_ref[:, cols] = parts[f]
        st = (resid_ref[:, cols].astype(F32) + parts[f]).astype(BF)
        stream[:, cols] = st
        sf = st.astype(F32)
        squares = squares + jnp.sum(sf * sf, axis=1, keepdims=True)
    inv = lax.rsqrt(squares / D + 1e-06)
    for f in range(4):
        cols = slice(f * 1024, f * 1024 + 1024)
        out = (stream[:, cols].astype(F32) * inv * gain_ref[:, cols]).astype(BF)
        norm[f // 2, :, (f % 2) * 1024 : (f % 2) * 1024 + 1024] = out
    gates = gate_ref[...]
    top = gates.astype(BF)
    rest = gates - top.astype(F32)
    middle = rest.astype(BF)
    low = (rest - middle.astype(F32)).astype(BF)
    lane = lax.broadcasted_iota(jnp.int32, (16, 128), 1)
    gates = jnp.where(lane < EXPERTS, top.astype(F32), jnp.where(lane < 2 * EXPERTS, middle.astype(F32), low.astype(F32)))
    for i in range(2):
        norm[i, :, HALF:] = gates.astype(BF)

    xf = (x0, x1, x2, x3, x4, x5)
    swap = remote(norm.at[1 - k], csh, ccs.at[0], ccr.at[0], sib)
    swap.start()
    own_tok = pl.ds(pl.multiple_of(k * 16, 16), 16)
    sib_tok = pl.ds(pl.multiple_of((1 - k) * 16, 16), 16)
    for f in range(6):
        xf[f][own6 + (own_tok, slice(0, USED[f]))] = norm[k, :, OFFS[f] : OFFS[f] + USED[f]]
    x4[own6 + (own_tok, slice(256, 384))] = norm[k, :, HALF:]
    swap.wait()
    for f in range(6):
        xf[f][own6 + (sib_tok, slice(0, USED[f]))] = csh[:, OFFS[f] : OFFS[f] + USED[f]]
    x4[own6 + (sib_tok, slice(256, 384))] = csh[:, HALF:]

    def ag_copy(f, s, j):
        idx = list(own6)
        for t in range(j):
            idx[CYCLE[(f + t) % 6]] = FULL
        if j >= 0:
            d = CYCLE[(f + j) % 6]
            idx[d] = 1 - own6[d]
        part = xf[f].at[tuple(idx)]
        return remote(part, part, ags.at[f, s, j + 1], agr.at[f, s, j + 1], ag_peer[CYCLE[(f + s) % 6]])

    for s in range(6):
        for f in range(6):
            ag_copy(f, s, -1).start()
    for s in range(6):
        for f in range(6):
            for j in range(-1, s):
                ag_copy(f, s, j).wait_recv()
            for t in range(s + 1, 6):
                ag_copy(f, t, s).start()
    for s in range(6):
        for f in range(6):
            for j in range(-1, s):
                ag_copy(f, s, j).wait_send()

    for cp in near_copies + far_copies:
        cp.wait()

    def chunk_bits(i):
        return (1 - own5[0] + i // 2) % 2, (1 - own5[1] + i % 2) % 2

    def chunk(i):
        b1, b0 = chunk_bits(i)
        return b1 * 2 + b0

    def chunk_rows(m):
        return pl.ds(pl.multiple_of(m * 256, 256), 256)

    def select(m):
        for g in range(2):
            pick = sel_ref[m * 2 + g]
            rows = pl.ds(pl.multiple_of(m * 256 + g * 128, 128), 128)
            for f in range(6):
                block = xf[f][m // 2, m % 2, g].reshape(256, WIDTHS[f])[:, : USED[f]]
                xs[rows, OFFS[f] : OFFS[f] + USED[f]] = jnp.dot(pick, block, preferred_element_type=F32).astype(BF)

    def partial_copy(m):
        return remote(psend.at[m], precv.at[m], pss.at[m], psr.at[m], sib)

    def other_units(m):
        a = xs[chunk_rows(m), :]
        psend[m, :, :FFS] = jnp.dot(a, wgs[...], preferred_element_type=F32).astype(BF)
        psend[m, :, FFS:] = jnp.dot(a, wus[...], preferred_element_type=F32).astype(BF)
        partial_copy(m).start()

    def hidden_cols(cc):
        return pl.ds(pl.multiple_of(cc * FFS, 128), FFS)

    def hidden_copy(m, cc, kind, to):
        part = hall.at[chunk_rows(m), hidden_cols(cc)]
        return remote(part, part, hss.at[kind, m], hsr.at[kind, m], to)

    def own_units(m):
        a = xs[chunk_rows(m), :]
        gate = jnp.dot(a, wgk[...], preferred_element_type=F32)
        upper = jnp.dot(a, wuk[...], preferred_element_type=F32)
        partial_copy(m).wait()
        gate = gate + precv[m, :, :FFS].astype(F32)
        upper = upper + precv[m, :, FFS:].astype(F32)
        hall[chunk_rows(m), hidden_cols(c)] = (gate / (1.0 + jnp.exp(-gate)) * upper).astype(BF)
        hidden_copy(m, c, 0, far).start()
        hidden_copy(m, c, 1, sib).start()

    def units(i):
        @pl.when(i < 4)
        def _():
            m = chunk(i)
            select(m)
            other_units(m)

        @pl.when(i > 0)
        def _():
            own_units(chunk(i - 1))

    pl.loop(0, 5)(units)
    far_c = (1 - zh) * 2 + k

    def half_copy(f, b1, b0):
        if f == 0:
            src, dst, sem = p2.at[0, b1, b0], r20.at[0, b0], b0
        elif f == 2:
            src, dst, sem = p2.at[2, b1, b0], r20.at[2, b1], b1
        elif f == 1:
            src, dst, sem = p2.at[1, b1, b0, 1 - own5[2]], r20.at[1, b1, b0], b1 * 2 + b0
        else:
            src, dst, sem = p2.at[3, b1, b0, :, 1 - own5[3]], r20.at[3, b1, b0], b1 * 2 + b0
        return remote(src, dst, has.at[f, sem], har.at[f, sem], rs_peer[RS_ORDER[f][0]])

    lane = lax.broadcasted_iota(jnp.int32, (256, 128), 1)
    my_lanes = jnp.logical_or(lane == e, jnp.logical_or(lane == e + EXPERTS, lane == e + 2 * EXPERTS))

    def down(i):
        b1, b0 = chunk_bits(i)
        m = b1 * 2 + b0
        hidden_copy(m, c, 1, sib).wait()
        hidden_copy(m, far_c, 2, sib).wait()
        a = hall[chunk_rows(m), :]
        weights = []
        for g in range(2):
            block = x4[b1, b0, g].reshape(256, 384)[:, 256:].astype(F32)
            weights.append(jnp.sum(jnp.where(my_lanes, block, 0.0), axis=1, keepdims=True))
        for f in range(4):
            cols = slice(f * 256, f * 256 + 256)
            out = jnp.dot(a, wdq[:, cols], preferred_element_type=F32).astype(BF)
            for g in range(2):
                tok = lax.dot_general(
                    sel_ref[m * 2 + g], out[g * 128 : g * 128 + 128], (((0,), (0,)), ((), ())),
                    preferred_element_type=F32,
                )
                tok = (tok * weights[g]).astype(BF)
                for yb in range(2):
                    for j in range(4):
                        zlo, zhi = ZMAP[j]
                        at = (yb * 4 + j) * 32
                        p2[f, b1, b0, g, yb, zlo, zhi * 32 : zhi * 32 + 32, :] = tok[at : at + 32]
            if f == 0:
                pl.when(i < 2)(lambda: half_copy(0, b1, b0).start())
            elif f == 2:
                pl.when(i % 2 == 0)(lambda: half_copy(2, b1, b0).start())
            else:
                half_copy(f, b1, b0).start()

    def spread(i):
        @pl.when(i < 4)
        def _():
            m = chunk(i)
            hidden_copy(m, c, 0, far).wait()
            hidden_copy(m, far_c, 2, sib).start()

        @pl.when(i > 0)
        def _():
            down(i - 1)

    pl.loop(0, 5)(spread)

    def wait_half(f):
        for b in range(2 if f % 2 == 0 else 4):
            if f == 0:
                half_copy(0, 1 - own5[0], b).wait()
            elif f == 2:
                half_copy(2, b, 1 - own5[1]).wait()
            else:
                half_copy(f, b // 2, b % 2).wait()

    def gram(j):
        cols = pl.ds(pl.multiple_of(j * 256, 256), 256)
        out = lax.dot_general(
            hall[:, hidden_cols(c)], hall[:, cols], (((0,), (0,)), ((), ())), preferred_element_type=F32
        )
        gram_ref[:, cols] = out

    pl.loop(0, 6)(gram)

    def nothing(f):
        return None

    run_rs(p2, recv2, s2s, s2r, wait_half, 4, nothing)
    final = []
    for i, (to, (flip_l, flip_h, flip_k)) in enumerate(
        (
            (sib, (0, 0, 1)), (peer_z1, (1, 0, 0)), (far, (0, 1, 0)), (peer_z3, (1, 1, 0)),
            (z1sib, (1, 0, 1)), (farsib, (0, 1, 1)), (z3sib, (1, 1, 1)),
        )
    ):
        to_l = 1 - zl if flip_l else zl
        to_c = (1 - zh if flip_h else zh) * 2 + (1 - k if flip_k else k)
        rows = pl.ds(pl.multiple_of(to_c * 16, 16), 16)
        cp = remote(p2.at[(FULL,) + own5[:4] + (to_l, rows)], frecv.at[zl, c], fss.at[i], fsr.at[i], to)
        cp.start()
        final.append(cp)
    rows = pl.ds(pl.multiple_of(c * 16, 16), 16)
    frecv[zl, c] = p2[(FULL,) + own5 + (rows,)]
    for cp in final:
        cp.wait()
    for cc in range(4):
        for f in range(4):
            cols = slice(cc * QUART + f * 256, cc * QUART + f * 256 + 256)
            routed = frecv[0, cc, f].astype(F32) + frecv[1, cc, f].astype(F32)
            mixed_ref[:, cols] = (stream[:, cols].astype(F32) + routed).astype(BF)


def fused(q, ow, resid, gain, gate, rank, keys, values, wg, wu, wd):
    dma = pltpu.SemaphoreType.DMA
    vm = pl.BlockSpec(memory_space=pltpu.VMEM)
    hbm = pl.BlockSpec(memory_space=pl.ANY)
    two = (2,) * 6

    def rs_scratch(rows, cols, steps):
        out = [pltpu.VMEM((4,) + (2,) * 5 + (rows, cols), BF)]
        for s in range(steps):
            out.append(pltpu.VMEM((4,) + (2,) * (4 - s) + (rows, cols), BF))
        return out

    scratch = (
        [pltpu.VMEM((512, 256), BF), pltpu.VMEM((16, D), BF), pltpu.VMEM((1, D), F32), pltpu.VMEM((16, 128), F32)]
        + [pltpu.VMEM((8, 1, 256), jnp.int32), dma((6,))]
        + [pltpu.VMEM((4, 512, HEAD_SIZE), BF), pltpu.VMEM((4, 512, 2 * HEAD_SIZE), BF), pltpu.VMEM((4, 256, 1), F32)]
        + [pltpu.VMEM((4, 256, 2 * HEAD_SIZE), F32), pltpu.VMEM((2,) * 5 + (16, 256), BF), pltpu.VMEM((8, 128, 256), BF)]
        + [pltpu.VMEM((256, D), BF)]
        + rs_scratch(16, 1024, 3)
        + [pltpu.VMEM((4, 3, 16, 1024), BF)]
        + [pltpu.VMEM((2, 16, WIDE), BF), pltpu.VMEM((16, D), BF), pltpu.VMEM((16, WIDE), BF)]
        + [pltpu.VMEM(two + (32, w), BF) for w in WIDTHS]
        + [pltpu.VMEM((HALF, FFS), BF)] * 4
        + [pltpu.VMEM((FF, QUART), BF), pltpu.VMEM((1024, HALF), BF)]
        + [pltpu.VMEM((4, 256, 2 * FFS), BF)] * 2
        + [pltpu.VMEM((1024, FF), BF)]
        + rs_scratch(64, 256, 4)
        + [pltpu.VMEM((2, 4, 4, 16, 256), BF)]
        + [dma((2,)), dma((3, 2)), dma((4, 2))]
        + [dma((4, 3)), dma((4, 3)), dma((4, 3)), dma((4, 3)), dma((5,)), dma((5,)), dma((3,)), dma((1,)), dma((1,))]
        + [dma((6, 6, 6)), dma((6, 6, 6)), dma((4,)), dma((4,)), dma((3, 4)), dma((3, 4))]
        + [dma((4, 4)), dma((4, 4)), dma((4, 4)), dma((4, 4)), dma((7,)), dma((7,))]
    )
    return pl.pallas_call(
        kernel,
        out_shape=(
            jax.ShapeDtypeStruct((16, D), BF),
            jax.ShapeDtypeStruct((16, D), F32),
            jax.ShapeDtypeStruct((FFS, FF), F32),
        ),
        in_specs=[hbm] * 11,
        out_specs=(vm, vm, vm),
        scratch_shapes=scratch,
        compiler_params=pltpu.CompilerParams(
            collective_id=0, has_side_effects=True, vmem_limit_bytes=62 * 2**20
        ),
        name="layer",
    )(q, ow, resid, gain, gate, rank, keys, values, wg, wu, wd)


def gray(a, axis):
    parts = [lax.slice_in_dim(a, i, i + 1, axis=axis) for i in GRAY]
    return jnp.concatenate(parts, axis=axis)


def gathered_order(a):
    rest = a.shape[1:]
    n = len(rest)
    a = a.reshape((2, 2, 4, 4, 2, 16) + rest)
    a = jnp.transpose(a, (2, 3, 0, 4, 1, 5) + tuple(range(6, 6 + n)))
    a = a.reshape((4, 4, 4, 32) + rest)
    for axis in range(3):
        a = gray(a, axis)
    return a.reshape((2048,) + rest)


def local(
    resid, query, keys, values, out_weight, post_gain, route_idx, gates, w_gate, w_up, w_down
):
    exp_pos = lax.axis_index("exp")
    block = lax.axis_index("ctx") * EXPERTS + exp_pos
    own_idx = lax.dynamic_slice_in_dim(route_idx, block * 16, 16, 0)
    expert = jnp.arange(128, dtype=jnp.int32)
    expert = jnp.where(expert < 3 * EXPERTS, expert % EXPERTS, -1)
    gate = jnp.sum(jnp.where(own_idx[:, :, None] == expert[None, None, :], gates[:, :, None], 0.0), axis=1)
    member = jnp.any(route_idx == exp_pos, axis=1)
    count = jnp.sum(member.astype(F32))
    member = gathered_order(member.astype(BF)).reshape(128, 16)
    before = (jnp.arange(16)[:, None] < jnp.arange(16)[None, :]).astype(BF)
    rank = jnp.dot(member, before, preferred_element_type=F32)
    rank = jnp.where(member > 0, rank, -1.0).astype(jnp.int32).reshape(8, 1, 256)
    mixed, attn_out, gram = fused(
        query, out_weight, resid, post_gain.reshape(1, D), gate, rank, keys, values, w_gate[0], w_up[0], w_down[0]
    )
    return (mixed, attn_out, (gram / count)[None])


def solution(mesh):
    placed = (
        P(("ctx", "exp"), None),
        P("ctx", "exp"),
        P("ctx", None),
        P("ctx", None),
        P("exp", None),
        P(),
        P(),
        P(("ctx", "exp"), None),
        P("exp", None, "ctx"),
        P("exp", None, "ctx"),
        P("exp", "ctx", None),
    )
    return jax.shard_map(
        local,
        mesh=mesh,
        in_specs=placed,
        out_specs=(P(("ctx", "exp"), None), P(("ctx", "exp"), None), P("exp", "ctx", None)),
        check_vma=False,
    )
```

```python
import functools
import math

import jax
import jax.numpy as jnp
from jax import lax
from jax.experimental import pallas as pl
from jax.experimental.pallas import tpu as pltpu
from jax.sharding import PartitionSpec as P

EXPERTS = 32
HEAD_SIZE = 128
D = 4096
FF = 1536
FFS = 384
HALF = D // 2
QUART = D // 4
MESH = pl.DeviceIdType.MESH
BF = jnp.bfloat16
F32 = jnp.float32

RS_ORDER = ((0, 2, 1, 3, 4), (2, 1, 3, 0, 4), (1, 3, 0, 2, 4), (3, 0, 2, 1, 4))
CYCLE = (0, 2, 4, 1, 3, 5)
WIDTHS = (384, 384, 384, 384, 384, 256)
USED = (384, 384, 384, 384, 256, 256)
OFFS = (0, 384, 768, 1152, 1536, 1792)
WIDE = HALF + 128
GRAY = (0, 1, 3, 2)
ZMAP = ((0, 0), (1, 0), (1, 1), (0, 1))
FULL = slice(None)


def block_bits(i, n):
    return [(i // (2 ** (n - 1 - j))) % 2 for j in range(n)]


def kernel(
    q_hbm, ow_hbm, resid_hbm, gain_hbm, gate_hbm, rank_hbm, keys_ref, values_ref, wg_ref, wu_ref, wd_ref,
    mixed_ref, attn_ref, gram_ref,
    q_ref, resid_ref, gain_ref, gate_ref, rank_ref, isem,
    kk, vv, top_s, acc_s, h_ref, sel_ref, ow_ref,
    p1, r10, r11, r12, r13, norm, stream, csh, x0, x1, x2, x3, x4, x5,
    wgk, wuk, wgs, wus, wdq, xs, psend, precv, hall, p2, r20, r21, r22, r23, frecv,
    kvl, kvs, kvr,
    s1s, s1r, t1s, t1r, wss, wsr, lsem, ccs, ccr, ags, agr, pss, psr, hss, hsr, has, har, s2s, s2r, fss, fsr,
):
    c = lax.axis_index("ctx")
    e = lax.axis_index("exp")
    x, y, zl, zh, k = e // 8, (e // 2) % 4, e % 2, c // 2, c % 2

    def dev(x_, y_, zl_, zh_, k_):
        return (zh_ * 2 + k_, x_ * 8 + y_ * 2 + zl_)

    def flip1(v):
        return v + 1 - 2 * (v % 2)

    peer_x = (dev(3 - x, y, zl, zh, k), dev(flip1(x), y, zl, zh, k))
    peer_y = (dev(x, 3 - y, zl, zh, k), dev(x, flip1(y), zl, zh, k))
    peer_z1 = dev(x, y, 1 - zl, zh, k)
    peer_z3 = dev(x, y, 1 - zl, 1 - zh, k)
    sib = dev(x, y, zl, zh, 1 - k)
    far = dev(x, y, zl, 1 - zh, k)
    farsib = dev(x, y, zl, 1 - zh, 1 - k)
    rs_peer = (peer_x[0], peer_x[1], peer_y[0], peer_y[1], peer_z1)
    diagonal = (
        dev(3 - x, y, 1 - zl, zh, k), dev(flip1(x), y, 1 - zl, zh, k),
        dev(x, 3 - y, 1 - zl, zh, k), dev(x, flip1(y), 1 - zl, zh, k),
    )
    z1sib, z3sib = dev(x, y, 1 - zl, zh, 1 - k), dev(x, y, 1 - zl, 1 - zh, 1 - k)
    ag_peer = (peer_x[0], peer_x[1], peer_y[0], peer_y[1], peer_z3, peer_z1)
    xb1, yb1 = x // 2, y // 2
    own5 = (xb1, (xb1 + x % 2) % 2, yb1, (yb1 + y % 2) % 2, zl)
    own6 = own5[:4] + (zh, (zh + zl) % 2)

    hbm_vmem = (
        (q_hbm, q_ref), (rank_hbm, rank_ref), (ow_hbm, ow_ref), (resid_hbm, resid_ref), (gain_hbm, gain_ref),
        (gate_hbm, gate_ref),
    )
    input_copies = [pltpu.make_async_copy(a, b, isem.at[i]) for i, (a, b) in enumerate(hbm_vmem)]
    barrier = pltpu.get_barrier_semaphore()
    partners = list(ag_peer) + [sib, far, farsib, z1sib, z3sib] + list(diagonal)
    for p in partners:
        pl.semaphore_signal(barrier, inc=1, device_id=p, device_id_type=MESH)
    pl.semaphore_wait(barrier, len(partners))

    def remote(src, dst, ss, rs, to):
        return pltpu.make_async_remote_copy(
            src_ref=src, dst_ref=dst, send_sem=ss, recv_sem=rs, device_id=to, device_id_type=MESH
        )

    head_cols = pl.ds(pl.multiple_of(x * HEAD_SIZE, HEAD_SIZE), HEAD_SIZE)
    kv_src = (keys_ref.at[:, head_cols], values_ref.at[:, head_cols])

    def kv_dst(cc, j):
        return vv.at[cc, :, 0:HEAD_SIZE] if j else kk.at[cc]

    def kv_copy(i, to, cc, j):
        return remote(kv_src[j], kv_dst(cc, j), kvs.at[i, j], kvr.at[cc, j], to)

    def kv_local(j):
        return pltpu.make_async_copy(kv_src[j], kv_dst(c, j), kvl.at[j])

    def kv_forward(j):
        return remote(kv_dst(k, j), kv_dst(k, j), kvs.at[2, j], kvr.at[k, j], sib)

    for j in range(2):

        @pl.when(zh == 0)
        def _():
            kv_copy(1, far, c, j).start()
            kv_copy(2, farsib, c, j).start()

    for j in range(2):

        @pl.when(k == 0)
        def _():
            kv_copy(0, sib, c, j).start()

        kv_local(j).start()

    for cp in input_copies:
        cp.start()

    other = pl.ds(pl.multiple_of((1 - k) * HALF, HALF), HALF)
    mine = pl.ds(pl.multiple_of(k * HALF, HALF), HALF)
    own_rows = pl.ds(pl.multiple_of(c * FFS, FFS), FFS)

    def quarter(cc):
        return pl.ds(pl.multiple_of(cc * QUART, QUART), QUART)

    near_copies = [
        remote(wg_ref.at[other], wgs, wss.at[0], wsr.at[0], sib),
        remote(wu_ref.at[other], wus, wss.at[1], wsr.at[1], sib),
        remote(wd_ref.at[:, quarter(zh * 2 + 1 - k)], wdq.at[own_rows], wss.at[2], wsr.at[2], sib),
        pltpu.make_async_copy(wg_ref.at[mine], wgk, lsem.at[0]),
        pltpu.make_async_copy(wu_ref.at[mine], wuk, lsem.at[1]),
        pltpu.make_async_copy(wd_ref.at[:, quarter(c)], wdq.at[own_rows], lsem.at[2]),
    ]
    far_copies = [
        remote(wd_ref.at[:, quarter((1 - zh) * 2 + k)], wdq.at[own_rows], wss.at[3], wsr.at[3], far),
        remote(wd_ref.at[:, quarter((1 - zh) * 2 + 1 - k)], wdq.at[own_rows], wss.at[4], wsr.at[4], farsib),
    ]

    @pl.when(zh == 1)
    def _():
        for cp in far_copies:
            cp.start()

    slot = lax.broadcasted_iota(jnp.int32, (128, 256), 0)
    token = lax.broadcasted_iota(jnp.int32, (128, 256), 1)
    place = jnp.where(slot // 8 == token // 16, slot % 8, -2)

    for cp in input_copies[:2]:
        cp.wait()

    def pick_slots(g):
        sel_ref[g] = jnp.where(place == rank_ref[g], 1.0, 0.0).astype(BF)

    pl.loop(0, 8)(pick_slots)
    for cc in range(4):
        vv[cc, :, HEAD_SIZE:] = jnp.ones((512, HEAD_SIZE), BF)
    scale = math.log2(math.e) / math.sqrt(HEAD_SIZE)
    trans = (((1,), (1,)), ((), ()))

    def queries(t):
        rows = slice(t * 128, t * 128 + 128)
        return jnp.concatenate([q_ref[rows, :HEAD_SIZE], q_ref[rows, HEAD_SIZE:]], axis=0)

    for j in range(2):
        kv_local(j).wait()
    for t in range(4):
        n = t * 128 + 128
        scores = lax.dot_general(queries(t), kk[c, :n], trans, preferred_element_type=F32)
        q_place = lax.rem(lax.broadcasted_iota(jnp.int32, (256, n), 0), 128) + t * 128
        scores = jnp.where(q_place >= lax.broadcasted_iota(jnp.int32, (256, n), 1), scores, -1e30)
        new = jnp.max(scores, axis=1, keepdims=True)
        w = jnp.exp2((scores - new) * scale).astype(BF)
        top_s[t] = new
        acc_s[t] = jnp.dot(w, vv[c, :n], preferred_element_type=F32)

    for cp in near_copies:
        cp.start()

    def key_block(i):
        cc = c - i

        for j in range(2):
            kv_copy(0, sib, cc, j).wait_recv()

        for t in range(4):
            scores = lax.dot_general(queries(t), kk[cc], trans, preferred_element_type=F32)
            old = top_s[t]
            new = jnp.maximum(old, jnp.max(scores, axis=1, keepdims=True))
            w = jnp.exp2((scores - new) * scale).astype(BF)
            fade = jnp.exp2((old - new) * scale)
            top_s[t] = new
            acc_s[t] = acc_s[t] * fade + jnp.dot(w, vv[cc], preferred_element_type=F32)

    pl.loop(1, c + 1)(key_block)

    @pl.when(zh == 0)
    def _():
        for cp in far_copies:
            cp.start()

    def head_tile(t):
        out = (acc_s[t, :, :HEAD_SIZE] / acc_s[t, :, HEAD_SIZE:]).astype(BF)
        b1 = t // 2
        b0 = (b1 + t % 2) % 2
        for hd in range(2):
            for yy in range(4):
                at = hd * 128 + yy * 32
                h_ref[b1, b0, yy // 2, (yy // 2 + yy) % 2, :, :, hd * 128 : hd * 128 + 128] = out[at : at + 32].reshape(2, 16, 128)

    pl.loop(0, 4)(head_tile)

    def rs_index(f, s, bit):
        order = RS_ORDER[f]
        idx = [FULL] * 5
        for d in order[:s]:
            idx[d] = own5[d]
        idx[order[s]] = bit
        return tuple(idx)

    def rs_copy(buf, recv, ss, rs, f, s):
        d = RS_ORDER[f][s]
        return remote(
            buf.at[(f,) + rs_index(f, s, 1 - own5[d])], recv[s].at[f], ss.at[f, s], rs.at[f, s], rs_peer[d]
        )

    def rs_add(buf, recv, f, s, bit):
        order = RS_ORDER[f]
        step = order[s + 1]
        left = sorted(order[s + 2 :])
        n = len(left)

        def one(i):
            bits = dict(zip(left, block_bits(i, n)))
            bits[step] = bit
            idx = list(own5)
            for d in bits:
                idx[d] = bits[d]
            idx = (f,) + tuple(idx)
            got = recv[s][(f,) + tuple(bits[d] for d in sorted(bits))]
            buf[idx] = (buf[idx].astype(F32) + got.astype(F32)).astype(BF)

        if n:
            pl.loop(0, 2**n)(one)
        else:
            one(0)

    recv1 = (r10, r11, r12)
    recv2 = (r20, r21, r22, r23)

    def project(f, bit):
        idx = rs_index(f, 0, bit)
        rows = h_ref[idx].reshape(256, 256)
        for t in range(2):
            cols = f * 1024 + t * 512
            out = jnp.dot(rows, ow_ref[:, cols : cols + 512], preferred_element_type=F32)
            p1[(f,) + idx + (FULL, slice(t * 512, t * 512 + 512))] = out.astype(BF).reshape(2, 2, 2, 2, 16, 512)

    for cp in input_copies[2:]:
        cp.wait()
    first = []
    for f in range(4):
        project(f, 1 - own5[RS_ORDER[f][0]])
        cp = rs_copy(p1, recv1, s1s, s1r, f, 0)
        cp.start()
        first.append(cp)

    for f in range(4):
        project(f, own5[RS_ORDER[f][0]])
    for j in range(2):

        @pl.when(zh == 0)
        def _():
            kv_copy(1, far, c, j).wait_send()
            kv_copy(2, farsib, c, j).wait_send()

        @pl.when(k == 0)
        def _():
            kv_copy(0, sib, c, j).wait_send()

    def run_rs(buf, recv, ss, rs, wait_first, steps, tail, beside):
        last = [None] * 4
        for s in range(steps):
            for f in range(4):
                if s == 0:
                    wait_first(f)
                else:
                    last[f].wait()
                d = RS_ORDER[f][s + 1]
                rs_add(buf, recv, f, s, 1 - own5[d])
                if s + 1 < steps:
                    last[f] = rs_copy(buf, recv, ss, rs, f, s + 1)
                    last[f].start()
                rs_add(buf, recv, f, s, own5[d])
                if s + 1 == steps:
                    tail(f)
            beside(s)

    tails = []

    def direct(f):
        d = RS_ORDER[f][3]
        for i, (to, flips) in enumerate(((rs_peer[d], (d,)), (peer_z1, (4,)), (diagonal[d], (d, 4)))):
            idx = tuple(1 - own5[j] if j in flips else own5[j] for j in range(5))
            cp = remote(p1.at[(f,) + idx], r13.at[f, i], t1s.at[f, i], t1r.at[f, i], to)
            cp.start()
            tails.append(cp)

    run_rs(p1, recv1, s1s, s1r, lambda f: first[f].wait(), 3, direct, lambda s: None)
    parts = []
    for f in range(4):
        for i in range(3):
            tails[f * 3 + i].wait()
        got = [r13[f, i].astype(F32) for i in range(3)]
        parts.append((p1[(f,) + own5].astype(F32) + got[0]) + (got[1] + got[2]))

    squares = jnp.zeros((16, 1), F32)
    for f in range(4):
        cols = slice(f * 1024, f * 1024 + 1024)
        attn_ref[:, cols] = parts[f]
        st = (resid_ref[:, cols].astype(F32) + parts[f]).astype(BF)
        stream[:, cols] = st
        sf = st.astype(F32)
        squares = squares + jnp.sum(sf * sf, axis=1, keepdims=True)
    inv = lax.rsqrt(squares / D + 1e-06)
    for f in range(4):
        cols = slice(f * 1024, f * 1024 + 1024)
        out = (stream[:, cols].astype(F32) * inv * gain_ref[:, cols]).astype(BF)
        norm[f // 2, :, (f % 2) * 1024 : (f % 2) * 1024 + 1024] = out
    gates = gate_ref[...]
    top = gates.astype(BF)
    rest = gates - top.astype(F32)
    middle = rest.astype(BF)
    low = (rest - middle.astype(F32)).astype(BF)
    lane = lax.broadcasted_iota(jnp.int32, (16, 128), 1)
    gates = jnp.where(lane < EXPERTS, top.astype(F32), jnp.where(lane < 2 * EXPERTS, middle.astype(F32), low.astype(F32)))
    for i in range(2):
        norm[i, :, HALF:] = gates.astype(BF)

    xf = (x0, x1, x2, x3, x4, x5)
    swap = remote(norm.at[1 - k], csh, ccs.at[0], ccr.at[0], sib)
    swap.start()
    own_tok = pl.ds(pl.multiple_of(k * 16, 16), 16)
    sib_tok = pl.ds(pl.multiple_of((1 - k) * 16, 16), 16)
    for f in range(6):
        xf[f][own6 + (own_tok, slice(0, USED[f]))] = norm[k, :, OFFS[f] : OFFS[f] + USED[f]]
    x4[own6 + (own_tok, slice(256, 384))] = norm[k, :, HALF:]
    swap.wait()
    for f in range(6):
        xf[f][own6 + (sib_tok, slice(0, USED[f]))] = csh[:, OFFS[f] : OFFS[f] + USED[f]]
    x4[own6 + (sib_tok, slice(256, 384))] = csh[:, HALF:]

    def ag_copy(f, s, j):
        idx = list(own6)
        for t in range(j):
            idx[CYCLE[(f + t) % 6]] = FULL
        if j >= 0:
            d = CYCLE[(f + j) % 6]
            idx[d] = 1 - own6[d]
        part = xf[f].at[tuple(idx)]
        return remote(part, part, ags.at[f, s, j + 1], agr.at[f, s, j + 1], ag_peer[CYCLE[(f + s) % 6]])

    for s in range(6):
        for f in range(6):
            ag_copy(f, s, -1).start()
    for s in range(6):
        for f in range(6):
            for j in range(-1, s):
                ag_copy(f, s, j).wait_recv()
            for t in range(s + 1, 6):
                ag_copy(f, t, s).start()
    for s in range(6):
        for f in range(6):
            for j in range(-1, s):
                ag_copy(f, s, j).wait_send()

    for cp in near_copies + far_copies:
        cp.wait()

    def chunk_bits(i):
        return (1 - own5[0] + i // 2) % 2, (1 - own5[1] + i % 2) % 2

    def chunk(i):
        b1, b0 = chunk_bits(i)
        return b1 * 2 + b0

    def chunk_rows(m):
        return pl.ds(pl.multiple_of(m * 256, 256), 256)

    def select(m):
        for g in range(2):
            pick = sel_ref[m * 2 + g]
            rows = pl.ds(pl.multiple_of(m * 256 + g * 128, 128), 128)
            for f in range(6):
                block = xf[f][m // 2, m % 2, g].reshape(256, WIDTHS[f])[:, : USED[f]]
                xs[rows, OFFS[f] : OFFS[f] + USED[f]] = jnp.dot(pick, block, preferred_element_type=F32).astype(BF)

    def partial_copy(m):
        return remote(psend.at[m], precv.at[m], pss.at[m], psr.at[m], sib)

    def other_units(m):
        a = xs[chunk_rows(m), :]
        psend[m, :, :FFS] = jnp.dot(a, wgs[...], preferred_element_type=F32).astype(BF)
        psend[m, :, FFS:] = jnp.dot(a, wus[...], preferred_element_type=F32).astype(BF)
        partial_copy(m).start()

    def hidden_cols(cc):
        return pl.ds(pl.multiple_of(cc * FFS, 128), FFS)

    def hidden_copy(m, cc, kind, to):
        part = hall.at[chunk_rows(m), hidden_cols(cc)]
        return remote(part, part, hss.at[kind, m], hsr.at[kind, m], to)

    def own_units(m):
        a = xs[chunk_rows(m), :]
        gate = jnp.dot(a, wgk[...], preferred_element_type=F32)
        upper = jnp.dot(a, wuk[...], preferred_element_type=F32)
        partial_copy(m).wait()
        gate = gate + precv[m, :, :FFS].astype(F32)
        upper = upper + precv[m, :, FFS:].astype(F32)
        hall[chunk_rows(m), hidden_cols(c)] = (gate / (1.0 + jnp.exp(-gate)) * upper).astype(BF)
        hidden_copy(m, c, 0, far).start()
        hidden_copy(m, c, 1, sib).start()

    def units(i):
        @pl.when(i < 4)
        def _():
            m = chunk(i)
            select(m)
            other_units(m)

        @pl.when(i > 0)
        def _():
            own_units(chunk(i - 1))

    pl.loop(0, 5)(units)
    far_c = (1 - zh) * 2 + k

    def half_copy(f, b1, b0):
        if f == 0:
            src, dst, sem = p2.at[0, b1, b0], r20.at[0, b0], b0
        elif f == 2:
            src, dst, sem = p2.at[2, b1, b0], r20.at[2, b1], b1
        elif f == 1:
            src, dst, sem = p2.at[1, b1, b0, 1 - own5[2]], r20.at[1, b1, b0], b1 * 2 + b0
        else:
            src, dst, sem = p2.at[3, b1, b0, :, 1 - own5[3]], r20.at[3, b1, b0], b1 * 2 + b0
        return remote(src, dst, has.at[f, sem], har.at[f, sem], rs_peer[RS_ORDER[f][0]])

    lane = lax.broadcasted_iota(jnp.int32, (256, 128), 1)
    my_lanes = jnp.logical_or(lane == e, jnp.logical_or(lane == e + EXPERTS, lane == e + 2 * EXPERTS))

    def down(i):
        b1, b0 = chunk_bits(i)
        m = b1 * 2 + b0
        hidden_copy(m, c, 1, sib).wait()
        hidden_copy(m, far_c, 2, sib).wait()
        a = hall[chunk_rows(m), :]
        weights = []
        for g in range(2):
            block = x4[b1, b0, g].reshape(256, 384)[:, 256:].astype(F32)
            weights.append(jnp.sum(jnp.where(my_lanes, block, 0.0), axis=1, keepdims=True))
        for f in range(4):
            cols = slice(f * 256, f * 256 + 256)
            out = jnp.dot(a, wdq[:, cols], preferred_element_type=F32).astype(BF)
            for g in range(2):
                tok = lax.dot_general(
                    sel_ref[m * 2 + g], out[g * 128 : g * 128 + 128], (((0,), (0,)), ((), ())),
                    preferred_element_type=F32,
                )
                tok = (tok * weights[g]).astype(BF)
                for yb in range(2):
                    for j in range(4):
                        zlo, zhi = ZMAP[j]
                        at = (yb * 4 + j) * 32
                        p2[f, b1, b0, g, yb, zlo, zhi * 32 : zhi * 32 + 32, :] = tok[at : at + 32]
            if f == 0:
                pl.when(i < 2)(lambda: half_copy(0, b1, b0).start())
            elif f == 2:
                pl.when(i % 2 == 0)(lambda: half_copy(2, b1, b0).start())
            else:
                half_copy(f, b1, b0).start()

    def spread(i):
        @pl.when(i < 4)
        def _():
            m = chunk(i)
            hidden_copy(m, c, 0, far).wait()
            hidden_copy(m, far_c, 2, sib).start()

        @pl.when(i > 0)
        def _():
            down(i - 1)

    pl.loop(0, 5)(spread)

    def wait_half(f):
        for b in range(2 if f % 2 == 0 else 4):
            if f == 0:
                half_copy(0, 1 - own5[0], b).wait()
            elif f == 2:
                half_copy(2, b, 1 - own5[1]).wait()
            else:
                half_copy(f, b // 2, b % 2).wait()

    def gram(j):
        cols = pl.ds(pl.multiple_of(j * 256, 256), 256)
        out = lax.dot_general(
            hall[:, hidden_cols(c)], hall[:, cols], (((0,), (0,)), ((), ())), preferred_element_type=F32
        )
        gram_ref[:, cols] = out

    pl.loop(0, 2)(gram)

    def nothing(f):
        return None

    def gram_part(s):
        if s < 2:
            pl.loop(s * 2 + 2, s * 2 + 4)(gram)

    run_rs(p2, recv2, s2s, s2r, wait_half, 4, nothing, gram_part)
    final = []
    for i, (to, (flip_l, flip_h, flip_k)) in enumerate(
        (
            (sib, (0, 0, 1)), (peer_z1, (1, 0, 0)), (far, (0, 1, 0)), (peer_z3, (1, 1, 0)),
            (z1sib, (1, 0, 1)), (farsib, (0, 1, 1)), (z3sib, (1, 1, 1)),
        )
    ):
        to_l = 1 - zl if flip_l else zl
        to_c = (1 - zh if flip_h else zh) * 2 + (1 - k if flip_k else k)
        rows = pl.ds(pl.multiple_of(to_c * 16, 16), 16)
        cp = remote(p2.at[(FULL,) + own5[:4] + (to_l, rows)], frecv.at[zl, c], fss.at[i], fsr.at[i], to)
        cp.start()
        final.append(cp)
    rows = pl.ds(pl.multiple_of(c * 16, 16), 16)
    frecv[zl, c] = p2[(FULL,) + own5 + (rows,)]
    for cp in final:
        cp.wait()
    for cc in range(4):
        for f in range(4):
            cols = slice(cc * QUART + f * 256, cc * QUART + f * 256 + 256)
            routed = frecv[0, cc, f].astype(F32) + frecv[1, cc, f].astype(F32)
            mixed_ref[:, cols] = (stream[:, cols].astype(F32) + routed).astype(BF)


def fused(q, ow, resid, gain, gate, rank, keys, values, wg, wu, wd):
    dma = pltpu.SemaphoreType.DMA
    vm = pl.BlockSpec(memory_space=pltpu.VMEM)
    hbm = pl.BlockSpec(memory_space=pl.ANY)
    two = (2,) * 6

    def rs_scratch(rows, cols, steps):
        out = [pltpu.VMEM((4,) + (2,) * 5 + (rows, cols), BF)]
        for s in range(steps):
            out.append(pltpu.VMEM((4,) + (2,) * (4 - s) + (rows, cols), BF))
        return out

    scratch = (
        [pltpu.VMEM((512, 256), BF), pltpu.VMEM((16, D), BF), pltpu.VMEM((1, D), F32), pltpu.VMEM((16, 128), F32)]
        + [pltpu.VMEM((8, 1, 256), jnp.int32), dma((6,))]
        + [pltpu.VMEM((4, 512, HEAD_SIZE), BF), pltpu.VMEM((4, 512, 2 * HEAD_SIZE), BF), pltpu.VMEM((4, 256, 1), F32)]
        + [pltpu.VMEM((4, 256, 2 * HEAD_SIZE), F32), pltpu.VMEM((2,) * 5 + (16, 256), BF), pltpu.VMEM((8, 128, 256), BF)]
        + [pltpu.VMEM((256, D), BF)]
        + rs_scratch(16, 1024, 3)
        + [pltpu.VMEM((4, 3, 16, 1024), BF)]
        + [pltpu.VMEM((2, 16, WIDE), BF), pltpu.VMEM((16, D), BF), pltpu.VMEM((16, WIDE), BF)]
        + [pltpu.VMEM(two + (32, w), BF) for w in WIDTHS]
        + [pltpu.VMEM((HALF, FFS), BF)] * 4
        + [pltpu.VMEM((FF, QUART), BF), pltpu.VMEM((1024, HALF), BF)]
        + [pltpu.VMEM((4, 256, 2 * FFS), BF)] * 2
        + [pltpu.VMEM((1024, FF), BF)]
        + rs_scratch(64, 256, 4)
        + [pltpu.VMEM((2, 4, 4, 16, 256), BF)]
        + [dma((2,)), dma((3, 2)), dma((4, 2))]
        + [dma((4, 3)), dma((4, 3)), dma((4, 3)), dma((4, 3)), dma((5,)), dma((5,)), dma((3,)), dma((1,)), dma((1,))]
        + [dma((6, 6, 6)), dma((6, 6, 6)), dma((4,)), dma((4,)), dma((3, 4)), dma((3, 4))]
        + [dma((4, 4)), dma((4, 4)), dma((4, 4)), dma((4, 4)), dma((7,)), dma((7,))]
    )
    return pl.pallas_call(
        kernel,
        out_shape=(
            jax.ShapeDtypeStruct((16, D), BF),
            jax.ShapeDtypeStruct((16, D), F32),
            jax.ShapeDtypeStruct((FFS, FF), F32),
        ),
        in_specs=[hbm] * 11,
        out_specs=(vm, vm, vm),
        scratch_shapes=scratch,
        compiler_params=pltpu.CompilerParams(
            collective_id=0, has_side_effects=True, vmem_limit_bytes=62 * 2**20
        ),
        name="layer",
    )(q, ow, resid, gain, gate, rank, keys, values, wg, wu, wd)


def gray(a, axis):
    parts = [lax.slice_in_dim(a, i, i + 1, axis=axis) for i in GRAY]
    return jnp.concatenate(parts, axis=axis)


def gathered_order(a):
    rest = a.shape[1:]
    n = len(rest)
    a = a.reshape((2, 2, 4, 4, 2, 16) + rest)
    a = jnp.transpose(a, (2, 3, 0, 4, 1, 5) + tuple(range(6, 6 + n)))
    a = a.reshape((4, 4, 4, 32) + rest)
    for axis in range(3):
        a = gray(a, axis)
    return a.reshape((2048,) + rest)


def local(
    resid, query, keys, values, out_weight, post_gain, route_idx, gates, w_gate, w_up, w_down
):
    exp_pos = lax.axis_index("exp")
    block = lax.axis_index("ctx") * EXPERTS + exp_pos
    own_idx = lax.dynamic_slice_in_dim(route_idx, block * 16, 16, 0)
    expert = jnp.arange(128, dtype=jnp.int32)
    expert = jnp.where(expert < 3 * EXPERTS, expert % EXPERTS, -1)
    gate = jnp.sum(jnp.where(own_idx[:, :, None] == expert[None, None, :], gates[:, :, None], 0.0), axis=1)
    member = jnp.any(route_idx == exp_pos, axis=1)
    count = jnp.sum(member.astype(F32))
    member = gathered_order(member.astype(BF)).reshape(128, 16)
    before = (jnp.arange(16)[:, None] < jnp.arange(16)[None, :]).astype(BF)
    rank = jnp.dot(member, before, preferred_element_type=F32)
    rank = jnp.where(member > 0, rank, -1.0).astype(jnp.int32).reshape(8, 1, 256)
    mixed, attn_out, gram = fused(
        query, out_weight, resid, post_gain.reshape(1, D), gate, rank, keys, values, w_gate[0], w_up[0], w_down[0]
    )
    return (mixed, attn_out, (gram / count)[None])


def solution(mesh):
    placed = (
        P(("ctx", "exp"), None),
        P("ctx", "exp"),
        P("ctx", None),
        P("ctx", None),
        P("exp", None),
        P(),
        P(),
        P(("ctx", "exp"), None),
        P("exp", None, "ctx"),
        P("exp", None, "ctx"),
        P("exp", "ctx", None),
    )
    return jax.shard_map(
        local,
        mesh=mesh,
        in_specs=placed,
        out_specs=(P(("ctx", "exp"), None), P(("ctx", "exp"), None), P("exp", "ctx", None)),
        check_vma=False,
    )
```
